32 devices in a mesh: blk: 8 (over y, x, core), head: 4 (over z).
Axes of the slice: x: 2, y: 2, z: 4, core: 2. Of those that a mesh axis runs over, the one named last changes fastest.
Arguments:
- query: bfloat16 [4096, 8192], P(('blk', 'head')), may hold values from -6 to 6
- key: bfloat16 [4096, 1024], P(('blk', 'head')), may hold values from -6 to 6
- value: bfloat16 [4096, 1024], P(('blk', 'head')), may hold values from -6 to 6
- output: bfloat16 [4096, 8192], P(('blk', 'head')), may hold values from -1.5 to 1.5
- out_grad: bfloat16 [4096, 8192], P(('blk', 'head')), may hold values from -6 to 6
- lse: float32 [4096, 64], P(('blk', 'head')), may hold values from 3.5 to 6
- doc_lengths: int32 [3], replicated, may hold values from 1 to 2048, as said below
- block_keep: int32 [32, 17], P('blk'), may hold values 0 or 1
Outputs:
- query_grad: bfloat16 [4096, 8192], P(('blk', 'head'))
- key_grad: bfloat16 [4096, 1024], P(('blk', 'head'))
- value_grad: bfloat16 [4096, 1024], P(('blk', 'head'))
The draws below stay inside these ranges and needn't reach their ends.
Inputs may be any that keep to these rules, and one draw needn't show every extreme that they name: `doc_lengths`: whole document lengths that sum to 4096; the sequence is cut into aligned windows of 2048 tokens, each but the last split into two documents, the last one document of exactly 2048.
All inputs are finite; a program needn't handle non-finite values. No bound on the sum of `block_keep` on one device may be relied on, other than what follows from the above.
Results may differ from the reference program's by a relative error of at most 0.015.
Values may be sent and summed in bfloat16 or wider, within the bound.
A program may use at most 128 MiB of HBM per device.

```python
import math
import jax
import jax.numpy as jnp
from jax import lax

HQ = 64
KVH = 8
HD = 128
TOK_BLK = 512
DOC_MAX = 2048
BLOCK = 128
TOKENS = 4096
NQB = 32
REACHB = 17


def draw_doc_lengths(key, part):
    windows = TOKENS // DOC_MAX
    cuts = jax.random.randint(key, (windows - 1,), 1, DOC_MAX, dtype=jnp.int32)
    pairs = jnp.stack([cuts, DOC_MAX - cuts], axis=1).reshape(-1)
    last = jnp.full((1,), DOC_MAX, jnp.int32)
    return jnp.concatenate([pairs, last]).astype(jnp.int32)


def set_ends(entries, rng, low, high):
    shape = entries.shape
    spot = [jax.random.randint(jax.random.fold_in(rng, axis), (), 0, shape[axis]) for axis in range(len(shape))]
    entries = entries.at[tuple(spot)].set(low)
    longest = shape.index(max(shape))
    spot[longest] = (spot[longest] + 1) % shape[longest]
    return entries.at[tuple(spot)].set(high)


def level_of(key, shape, shards, least, top_value):
    level, own = 1.0, jax.random.fold_in(key, 6)
    for position, shards_of in shards:
        draws = jnp.exp(jax.random.uniform(jax.random.fold_in(own, position), (shards_of,), jnp.float32, least / len(shards), top_value / len(shards)))
        level = level * jnp.repeat(draws, shape[position] // shards_of).reshape([-1 if axis == position else 1 for axis in range(len(shape))])
    return level


def centred(rng, shape, deviation, limit, cuts=(), held_as=jnp.bfloat16):
    factor_of = level_of(rng, shape, cuts, -0.22, 0.18) if cuts else 1.0
    array = jax.random.normal(rng, shape, jnp.float32) * deviation * factor_of
    return jnp.minimum(jnp.maximum(array, -limit), limit).astype(held_as)


def setup_inputs(seed: int = 0) -> dict:
    seeds = jax.random.split(jax.random.key(seed), 9)
    return {
        "query": centred(seeds[0], (TOKENS, HQ * HD), 1.0, 6.0, ((0, 32),)),
        "key": centred(seeds[1], (TOKENS, KVH * HD), 1.0, 6.0, ((0, 32),)),
        "value": centred(seeds[2], (TOKENS, KVH * HD), 1.0, 6.0, ((0, 32),)),
        "output": centred(seeds[3], (TOKENS, HQ * HD), 0.25, 1.5, ((0, 32),)),
        "out_grad": centred(seeds[4], (TOKENS, HQ * HD), 1.0, 6.0, ((0, 32),)),
        "lse": jnp.clip(3.5 + 2.5 * jax.random.uniform(seeds[5], (TOKENS, HQ), jnp.float32) ** level_of(seeds[5], (TOKENS, HQ), ((0, 32),), -0.2, 0.2), 3.5, 6.0),
        "doc_lengths": draw_doc_lengths(jax.random.fold_in(seeds[8], 71), 0),
        "block_keep": set_ends((jax.random.randint(seeds[7], (NQB, REACHB), 0, 4) < 3).astype(jnp.int32), jax.random.fold_in(seeds[7], 1), 0, 1),
    }


def doc_index(positions, starts):
    return lax.optimization_barrier(jnp.sum((positions[:, None] >= starts[None, :]).astype(jnp.int32), axis=1)) - 1

def block_table(first_query, first_key, rows, count_query, count_key):
    query_blocks = first_query // BLOCK + jnp.arange(count_query // BLOCK, dtype=jnp.int32)
    key_blocks = first_key // BLOCK + jnp.arange(count_key // BLOCK, dtype=jnp.int32)
    distance = query_blocks[:, None] - key_blocks[None, :]
    offsets = jnp.arange(rows.shape[1], dtype=jnp.int32)
    table = lax.optimization_barrier(jnp.sum(jnp.where(distance[:, :, None] == offsets[None, None, :], rows[:, None, :], 0), axis=2)) > 0
    return jnp.repeat(jnp.repeat(table, BLOCK, axis=0), BLOCK, axis=1)

def reference(query, key, value, output, out_grad, lse, doc_lengths, block_keep):
    f32 = jnp.float32
    group = HQ // KVH
    span = DOC_MAX + TOK_BLK
    scale = 1.0 / math.sqrt(HD)
    starts = (jnp.cumsum(doc_lengths) - doc_lengths).astype(jnp.int32)
    query4 = query.reshape(TOKENS, KVH, group, HD)
    grad4 = out_grad.reshape(TOKENS, KVH, group, HD)
    delta = lax.optimization_barrier(jnp.sum(grad4.astype(f32) * output.reshape(TOKENS, KVH, group, HD).astype(f32), axis=3))
    lse3 = lse.reshape(TOKENS, KVH, group)
    padding = jnp.zeros((DOC_MAX, KVH, HD), key.dtype)
    key_pad = jnp.concatenate([padding, key.reshape(TOKENS, KVH, HD)], axis=0)
    value_pad = jnp.concatenate([padding, value.reshape(TOKENS, KVH, HD)], axis=0)

    def one_head(parts):
        q_head, g_head, lse_head, delta_head, k_head, v_head = parts

        def tile(carry, index):
            dk_acc, dv_acc = carry
            first = (index * TOK_BLK).astype(jnp.int32)
            q_tile = lax.dynamic_slice_in_dim(q_head, first, TOK_BLK, 0).astype(f32)
            g_tile = lax.dynamic_slice_in_dim(g_head, first, TOK_BLK, 0).astype(f32)
            lse_tile = lax.dynamic_slice_in_dim(lse_head, first, TOK_BLK, 0)
            delta_tile = lax.dynamic_slice_in_dim(delta_head, first, TOK_BLK, 0)
            k_tile = lax.dynamic_slice_in_dim(k_head, first, span, 0).astype(f32)
            v_tile = lax.dynamic_slice_in_dim(v_head, first, span, 0).astype(f32)
            q_pos = first + jnp.arange(TOK_BLK, dtype=jnp.int32)
            k_pos = first - DOC_MAX + jnp.arange(span, dtype=jnp.int32)
            same = doc_index(q_pos, starts)[:, None] == doc_index(k_pos, starts)[None, :]
            causal = k_pos[None, :] <= q_pos[:, None]
            rows = lax.dynamic_slice_in_dim(block_keep, first // BLOCK, TOK_BLK // BLOCK, 0)
            allowed = same & causal & block_table(first, first - DOC_MAX, rows, TOK_BLK, span)
            scores = jnp.einsum('tgd,sd->gts', q_tile, k_tile) * scale
            probs = jnp.where(allowed[None], jnp.exp(scores - lse_tile.T[:, :, None]), 0.0)
            dprobs = jnp.einsum('tgd,sd->gts', g_tile, v_tile)
            dscores = probs * (dprobs - delta_tile.T[:, :, None])
            probs_b = lax.optimization_barrier(probs.astype(jnp.bfloat16)).astype(f32)
            dscores_b = lax.optimization_barrier(dscores.astype(jnp.bfloat16)).astype(f32)
            dv_part = jnp.einsum('gts,tgd->sd', probs_b, g_tile)
            dk_part = jnp.einsum('gts,tgd->sd', dscores_b, q_tile)
            dq_tile = (jnp.einsum('gts,sd->tgd', dscores_b, k_tile) * scale).astype(jnp.bfloat16)
            window_k = lax.dynamic_slice_in_dim(dk_acc, first, span, 0) + dk_part
            window_v = lax.dynamic_slice_in_dim(dv_acc, first, span, 0) + dv_part
            dk_acc = lax.dynamic_update_slice_in_dim(dk_acc, window_k, first, 0)
            dv_acc = lax.dynamic_update_slice_in_dim(dv_acc, window_v, first, 0)
            return ((dk_acc, dv_acc), dq_tile)
        zeros = jnp.zeros((TOKENS + DOC_MAX, HD), f32)
        (dk_acc, dv_acc), dq_tiles = lax.scan(tile, (zeros, zeros), jnp.arange(TOKENS // TOK_BLK, dtype=jnp.int32))
        dq_head = dq_tiles.reshape(TOKENS, group, HD)
        dk_head = (dk_acc[DOC_MAX:] * scale).astype(jnp.bfloat16)
        dv_head = dv_acc[DOC_MAX:].astype(jnp.bfloat16)
        return (dq_head, dk_head, dv_head)
    parts = (query4.transpose(1, 0, 2, 3), grad4.transpose(1, 0, 2, 3), lse3.transpose(1, 0, 2), delta.transpose(1, 0, 2), key_pad.transpose(1, 0, 2), value_pad.transpose(1, 0, 2))
    dq_all, dk_all, dv_all = lax.map(one_head, parts)
    query_grad = dq_all.transpose(1, 0, 2, 3).reshape(TOKENS, HQ * HD)
    key_grad = dk_all.transpose(1, 0, 2).reshape(TOKENS, KVH * HD)
    value_grad = dv_all.transpose(1, 0, 2).reshape(TOKENS, KVH * HD)
    return (query_grad, key_grad, value_grad)
```

```python
import functools
import math

import jax
import jax.numpy as jnp
from jax import lax
from jax.experimental import pallas as pl
from jax.experimental.pallas import tpu as pltpu
from jax.sharding import PartitionSpec as P

KVH = 8
HD = 128
DOC_MAX = 2048
BLOCK = 128
LOG2E = 1.4426950408889634
FAR = 1 << 20


def attention_kernel(
    range_rows, info, starts, keep, qg_ref, stats_ref, kv_ref, dq_ref, dkv_ref,
    k_all, v_all, kt_all, dk_acc, dv_acc, dqt_acc, blocks,
):
    f32 = jnp.float32
    step = pl.program_id(0)
    steps = pl.num_programs(0)
    parts, ranges, _, rows, _ = kv_ref.shape
    group = qg_ref.shape[3] // HD
    total = group * rows
    width = min(total, 256)
    scale = 1.0 / math.sqrt(HD)
    offset = info[0]

    @pl.when(step == 0)
    def _():
        for t in range(ranges):
            for z in range(parts):
                first = (t * parts + z) * rows
                k_all[first : first + rows, :] = kv_ref[z, t, 0]
                v_all[first : first + rows, :] = kv_ref[z, t, 1]
        for first in range(0, k_all.shape[0], 256):
            piece = k_all[first : first + 256, :].astype(f32)
            kt_all[:, first : first + 256] = piece.T.astype(jnp.bfloat16)
        dk_acc[...] = jnp.zeros_like(dk_acc)
        dv_acc[...] = jnp.zeros_like(dv_acc)

    first_query = step * range_rows + offset
    query_block = first_query // BLOCK

    def doc_start(position):
        found = jnp.zeros_like(position)
        for d in range(starts.shape[0]):
            found = jnp.maximum(found, jnp.where(starts[d] <= position, starts[d], 0))
        return found

    first_start = doc_start(first_query)

    def list_block(j, count):
        kept = keep[query_block, query_block - j] == 1
        reaches = (j + 1) * BLOCK > first_start
        blocks[count] = j
        return count + jnp.where(kept & reaches, 1, 0)

    count = lax.fori_loop(0, query_block + 1, list_block, jnp.int32(0))
    blocks[count] = -1

    dqt_acc[...] = jnp.zeros_like(dqt_acc)
    row_query = first_query + lax.broadcasted_iota(jnp.int32, (1, width), 1) % rows
    row_start = doc_start(row_query)
    queries = [qg_ref[0, 0, :, h * HD : (h + 1) * HD] for h in range(group)]
    grads = [qg_ref[0, 1, :, h * HD : (h + 1) * HD] for h in range(group)]
    queries = jnp.concatenate(queries, axis=0)
    grads = jnp.concatenate(grads, axis=0)

    def pair(p, _):
        j0 = blocks[2 * p]
        j1 = blocks[2 * p + 1]
        j1_first = jnp.where(j1 < 0, FAR, j1 * BLOCK)
        at0 = pl.ds(pl.multiple_of(j0 * BLOCK, BLOCK), BLOCK)
        at1 = pl.ds(pl.multiple_of(jnp.maximum(j1, 0) * BLOCK, BLOCK), BLOCK)
        keys = jnp.concatenate([k_all[at0, :], k_all[at1, :]], axis=0)
        values = jnp.concatenate([v_all[at0, :], v_all[at1, :]], axis=0)
        keys_t = jnp.concatenate([kt_all[:, at0], kt_all[:, at1]], axis=1)
        line = lax.broadcasted_iota(jnp.int32, (2 * BLOCK, width), 0)
        key_pos = jnp.where(line < BLOCK, line + j0 * BLOCK, line - BLOCK + j1_first)
        allowed = (key_pos <= row_query) & (key_pos >= row_start)
        probs_all, dscores_all = [], []
        for first in range(0, total, width):
            q = queries[first : first + width]
            g = grads[first : first + width]
            nt = (((1,), (1,)), ((), ()))
            s = lax.dot_general(keys, q, nt, preferred_element_type=f32)
            dp = lax.dot_general(values, g, nt, preferred_element_type=f32)
            lse = stats_ref[0, 0:1, first : first + width]
            delta = stats_ref[0, 1:2, first : first + width]
            probs = jnp.where(allowed, jnp.exp2(s * (scale * LOG2E) - lse), 0.0)
            dscores = probs * (dp - delta)
            probs_all.append(probs.astype(jnp.bfloat16))
            dscores_all.append(dscores.astype(jnp.bfloat16))
        probs_all = jnp.concatenate(probs_all, axis=1)
        dscores_all = jnp.concatenate(dscores_all, axis=1)
        dv = jnp.dot(probs_all, grads, preferred_element_type=f32)
        dk = jnp.dot(dscores_all, queries, preferred_element_type=f32)
        dqt_acc[...] += jnp.dot(keys_t, dscores_all, preferred_element_type=f32)
        dv_acc[at0, :] += dv[:BLOCK]
        dk_acc[at0, :] += dk[:BLOCK]
        dv_acc[at1, :] += dv[BLOCK:]
        dk_acc[at1, :] += dk[BLOCK:]
        return 0

    lax.fori_loop(0, (count + 1) // 2, pair, 0)
    for first in range(0, total, width):
        dq = (dqt_acc[:, first : first + width] * scale).T.astype(jnp.bfloat16)
        for h in range(width // rows):
            head = first // rows + h
            dq_ref[0, :, head * HD : (head + 1) * HD] = dq[h * rows : (h + 1) * rows]

    @pl.when(step == steps - 1)
    def _():
        for t in range(ranges):
            for z in range(parts):
                first = (t * parts + z) * rows
                dkv_ref[z, t, 0] = (dk_acc[first : first + rows, :] * scale).astype(jnp.bfloat16)
                dkv_ref[z, t, 1] = dv_acc[first : first + rows, :].astype(jnp.bfloat16)


def attention(info, starts, keep, qg, stats, kv, range_rows):
    ranges, _, rows, columns = qg.shape
    parts = kv.shape[0]
    span = parts * ranges * rows
    total = rows * columns // HD
    smem = pl.BlockSpec(memory_space=pltpu.SMEM)
    f32, bf16 = jnp.float32, jnp.bfloat16
    return pl.pallas_call(
        functools.partial(attention_kernel, range_rows),
        grid=(ranges,),
        out_shape=(
            jax.ShapeDtypeStruct((ranges, rows, columns), bf16),
            jax.ShapeDtypeStruct(kv.shape, bf16),
        ),
        in_specs=[
            smem, smem, smem,
            pl.BlockSpec((1, 2, rows, columns), lambda t: (t, 0, 0, 0)),
            pl.BlockSpec((1, 2, total), lambda t: (t, 0, 0)),
            pl.BlockSpec(kv.shape, lambda t: (0, 0, 0, 0, 0)),
        ],
        out_specs=(
            pl.BlockSpec((1, rows, columns), lambda t: (t, 0, 0)),
            pl.BlockSpec(kv.shape, lambda t: (0, 0, 0, 0, 0)),
        ),
        scratch_shapes=[
            pltpu.VMEM((span, HD), bf16),
            pltpu.VMEM((span, HD), bf16),
            pltpu.VMEM((HD, span), bf16),
            pltpu.VMEM((span, HD), f32),
            pltpu.VMEM((span, HD), f32),
            pltpu.VMEM((HD, total), f32),
            pltpu.SMEM((64,), jnp.int32),
        ],
        compiler_params=pltpu.CompilerParams(vmem_limit_bytes=40 * 1024 * 1024),
        cost_estimate=pl.CostEstimate(
            flops=5 * 2 * total * span * HD * ranges // 2,
            bytes_accessed=3 * ranges * rows * columns * 2 + 4 * span * HD * 2,
            transcendentals=total * span * ranges // 2,
        ),
    )(info, starts, keep, qg, stats, kv)


def shards(query, key, value, output, out_grad, lse, doc_lengths, block_keep):
    f32, bf16 = jnp.float32, jnp.bfloat16
    rows = query.shape[0]
    parts = lax.axis_size("head")
    range_rows = rows * parts
    ranges = DOC_MAX // range_rows
    blks = lax.axis_size("blk")
    groups = [[w + r for r in range(ranges)] for w in range(0, blks, ranges)]
    chunks = KVH // ranges
    heads = query.shape[1] // HD
    group = heads // KVH
    columns = group * HD
    sub = lax.axis_index("head")
    window = lax.axis_index("blk") // ranges

    def swap(array):
        return lax.all_to_all(array, "blk", 0, 0, axis_index_groups=groups)

    starts = (jnp.cumsum(doc_lengths) - doc_lengths - window * DOC_MAX).astype(jnp.int32)
    info = jnp.full((1,), sub * rows, jnp.int32)
    keep = lax.all_gather(block_keep, "blk", axis_index_groups=groups, tiled=True)

    q5 = query.reshape(rows, ranges, chunks, columns)
    g5 = out_grad.reshape(rows, ranges, chunks, columns)
    k5 = key.reshape(rows, ranges, chunks, HD)
    v5 = value.reshape(rows, ranges, chunks, HD)
    kv_in, qg_in = [], []
    for c in range(chunks):
        kv = jnp.stack([k5[:, :, c], v5[:, :, c]], axis=0).transpose(2, 0, 1, 3)
        kv_in.append(lax.all_gather(swap(kv), "head"))
        qg = jnp.stack([q5[:, :, c], g5[:, :, c]], axis=0).transpose(2, 0, 1, 3)
        qg_in.append(swap(qg))
    delta = jnp.sum(
        out_grad.reshape(rows, heads, HD).astype(f32) * output.reshape(rows, heads, HD).astype(f32),
        axis=2,
    )
    stats = jnp.stack([lse * LOG2E, delta], axis=0)
    stats = stats.reshape(2, rows, ranges, chunks, group).transpose(2, 3, 0, 4, 1)
    stats = swap(stats.reshape(ranges, chunks, 2, group * rows))

    dq_out, dkv_out = [], []
    for c in range(chunks):
        dq, dkv = attention(info, starts, keep, qg_in[c], stats[:, c], kv_in[c], range_rows)
        dq_out.append(swap(dq))
        partial = lax.all_to_all(dkv, "head", 0, 0)
        summed = jnp.sum(partial.astype(f32), axis=0).astype(bf16)
        dkv_out.append(swap(summed))
    query_grad = jnp.stack(dq_out, axis=1).transpose(2, 0, 1, 3).reshape(rows, heads * HD)
    dkv = jnp.stack(dkv_out, axis=1)
    key_grad = dkv[:, :, 0].transpose(2, 0, 1, 3).reshape(rows, KVH * HD)
    value_grad = dkv[:, :, 1].transpose(2, 0, 1, 3).reshape(rows, KVH * HD)
    return (query_grad, key_grad, value_grad)


def solution(mesh):
    tokens = P(("blk", "head"), None)
    in_specs = (tokens, tokens, tokens, tokens, tokens, tokens, P(), P("blk", None))
    out_specs = (tokens, tokens, tokens)
    return jax.shard_map(shards, mesh=mesh, in_specs=in_specs, out_specs=out_specs, check_vma=False)
```

```python
import functools
import math

import jax
import jax.numpy as jnp
from jax import lax
from jax.experimental import pallas as pl
from jax.experimental.pallas import tpu as pltpu
from jax.sharding import PartitionSpec as P

KVH = 8
HD = 128
DOC_MAX = 2048
BLOCK = 128
LOG2E = 1.4426950408889634
FAR = 1 << 20
MESH = pl.DeviceIdType.MESH


def attention_kernel(
    range_rows, info, starts, keep, qg_ref, stats_ref, kv_ref, dq_ref, dkv_ref,
    k_all, v_all, kt_all, dk_acc, dv_acc, dqt_acc, blocks,
):
    f32 = jnp.float32
    step = pl.program_id(1)
    steps = pl.num_programs(1)
    parts, ranges, _, rows, _ = kv_ref.shape
    group = qg_ref.shape[3] // HD
    total = group * rows
    width = min(total, 256)
    scale = 1.0 / math.sqrt(HD)
    offset = info[0]

    @pl.when(step == 0)
    def _():
        for t in range(ranges):
            for z in range(parts):
                first = (t * parts + z) * rows
                k_all[first : first + rows, :] = kv_ref[z, t, 0]
                v_all[first : first + rows, :] = kv_ref[z, t, 1]
        for first in range(0, k_all.shape[0], 256):
            piece = k_all[first : first + 256, :].astype(f32)
            kt_all[:, first : first + 256] = piece.T.astype(jnp.bfloat16)
        dk_acc[...] = jnp.zeros_like(dk_acc)
        dv_acc[...] = jnp.zeros_like(dv_acc)

    first_query = step * range_rows + offset
    query_block = first_query // BLOCK

    def doc_start(position):
        found = jnp.zeros_like(position)
        for d in range(starts.shape[0]):
            found = jnp.maximum(found, jnp.where(starts[d] <= position, starts[d], 0))
        return found

    first_start = doc_start(first_query)

    def list_block(j, count):
        kept = keep[step, query_block - step * (range_rows // BLOCK), query_block - j] == 1
        reaches = (j + 1) * BLOCK > first_start
        blocks[count] = j
        return count + jnp.where(kept & reaches, 1, 0)

    count = lax.fori_loop(0, query_block + 1, list_block, jnp.int32(0))
    blocks[count] = -1

    dqt_acc[...] = jnp.zeros_like(dqt_acc)
    row_query = first_query + lax.broadcasted_iota(jnp.int32, (1, width), 1) % rows
    row_start = doc_start(row_query)
    queries = [qg_ref[0, 0, :, h * HD : (h + 1) * HD] for h in range(group)]
    grads = [qg_ref[0, 1, :, h * HD : (h + 1) * HD] for h in range(group)]
    queries = jnp.concatenate(queries, axis=0)
    grads = jnp.concatenate(grads, axis=0)

    def pair(p, _):
        j0 = blocks[2 * p]
        j1 = blocks[2 * p + 1]
        j1_first = jnp.where(j1 < 0, FAR, j1 * BLOCK)
        at0 = pl.ds(pl.multiple_of(j0 * BLOCK, BLOCK), BLOCK)
        at1 = pl.ds(pl.multiple_of(jnp.maximum(j1, 0) * BLOCK, BLOCK), BLOCK)
        keys = jnp.concatenate([k_all[at0, :], k_all[at1, :]], axis=0)
        values = jnp.concatenate([v_all[at0, :], v_all[at1, :]], axis=0)
        keys_t = jnp.concatenate([kt_all[:, at0], kt_all[:, at1]], axis=1)
        line = lax.broadcasted_iota(jnp.int32, (2 * BLOCK, width), 0)
        key_pos = jnp.where(line < BLOCK, line + j0 * BLOCK, line - BLOCK + j1_first)
        allowed = (key_pos <= row_query) & (key_pos >= row_start)
        probs_all, dscores_all = [], []
        for first in range(0, total, width):
            q = queries[first : first + width]
            g = grads[first : first + width]
            nt = (((1,), (1,)), ((), ()))
            s = lax.dot_general(keys, q, nt, preferred_element_type=f32)
            dp = lax.dot_general(values, g, nt, preferred_element_type=f32)
            lse = stats_ref[0, 0, 0:1, first : first + width]
            delta = stats_ref[0, 0, 1:2, first : first + width]
            probs = jnp.where(allowed, jnp.exp2(s * (scale * LOG2E) - lse), 0.0)
            dscores = probs * (dp - delta)
            probs_all.append(probs.astype(jnp.bfloat16))
            dscores_all.append(dscores.astype(jnp.bfloat16))
        probs_all = jnp.concatenate(probs_all, axis=1)
        dscores_all = jnp.concatenate(dscores_all, axis=1)
        dv = jnp.dot(probs_all, grads, preferred_element_type=f32)
        dk = jnp.dot(dscores_all, queries, preferred_element_type=f32)
        dqt_acc[...] += jnp.dot(keys_t, dscores_all, preferred_element_type=f32)
        dv_acc[at0, :] += dv[:BLOCK]
        dk_acc[at0, :] += dk[:BLOCK]
        dv_acc[at1, :] += dv[BLOCK:]
        dk_acc[at1, :] += dk[BLOCK:]
        return 0

    lax.fori_loop(0, (count + 1) // 2, pair, 0)
    for first in range(0, total, width):
        dq = (dqt_acc[:, first : first + width] * scale).T.astype(jnp.bfloat16)
        for h in range(width // rows):
            head = first // rows + h
            dq_ref[0, :, head * HD : (head + 1) * HD] = dq[h * rows : (h + 1) * rows]

    @pl.when(step == steps - 1)
    def _():
        for t in range(ranges):
            for z in range(parts):
                first = (t * parts + z) * rows
                dkv_ref[z, t, 0] = (dk_acc[first : first + rows, :] * scale).astype(jnp.bfloat16)
                dkv_ref[z, t, 1] = dv_acc[first : first + rows, :].astype(jnp.bfloat16)


def attention(info, starts, keep, qg, stats, kv, range_rows):
    ranges, _, rows, columns = qg.shape
    parts = kv.shape[0]
    chunks = stats.shape[1]
    columns = columns // chunks
    span = parts * ranges * rows
    total = rows * columns // HD
    smem = pl.BlockSpec(memory_space=pltpu.SMEM)
    f32, bf16 = jnp.float32, jnp.bfloat16
    kv_spec = pl.BlockSpec((parts, ranges, 2, rows, HD), lambda c, t: (0, 0, 0, 0, c))
    return pl.pallas_call(
        functools.partial(attention_kernel, range_rows),
        grid=(chunks, ranges),
        out_shape=(
            jax.ShapeDtypeStruct((ranges, rows, columns * chunks), bf16),
            jax.ShapeDtypeStruct(kv.shape, bf16),
        ),
        in_specs=[
            smem, smem, smem,
            pl.BlockSpec((1, 2, rows, columns), lambda c, t: (t, 0, 0, c)),
            pl.BlockSpec((1, 1, 2, total), lambda c, t: (t, c, 0, 0)),
            kv_spec,
        ],
        out_specs=(pl.BlockSpec((1, rows, columns), lambda c, t: (t, 0, c)), kv_spec),
        scratch_shapes=[
            pltpu.VMEM((span, HD), bf16),
            pltpu.VMEM((span, HD), bf16),
            pltpu.VMEM((HD, span), bf16),
            pltpu.VMEM((span, HD), f32),
            pltpu.VMEM((span, HD), f32),
            pltpu.VMEM((HD, total), f32),
            pltpu.SMEM((64,), jnp.int32),
        ],
        compiler_params=pltpu.CompilerParams(vmem_limit_bytes=40 * 1024 * 1024),
        cost_estimate=pl.CostEstimate(
            flops=5 * 2 * total * span * HD * ranges * chunks // 2,
            bytes_accessed=(3 * ranges * rows * columns * 2 + 4 * span * HD * 2) * chunks,
            transcendentals=total * span * ranges * chunks // 2,
        ),
    )(info, starts, keep, qg, stats, kv)


def place(ranges):
    blk, sub = lax.axis_index("blk"), lax.axis_index("head")
    mine = blk % ranges
    return blk - mine, mine, sub


def enter(base, mine, sub, ranges, parts):
    barrier = pltpu.get_barrier_semaphore()
    for d in range(1, ranges):
        peer = (base + (mine + d) % ranges, sub)
        pl.semaphore_signal(barrier, inc=1, device_id=peer, device_id_type=MESH)
    for d in range(1, parts):
        peer = (base + mine, (sub + d) % parts)
        pl.semaphore_signal(barrier, inc=1, device_id=peer, device_id_type=MESH)
    pl.semaphore_wait(barrier, ranges - 1 + parts - 1)


def exchange_in_kernel(
    ranges, parts, query, key, value, output, out_grad, lse_t, block_keep,
    qg, stats, kv, keep,
    g_vmem, o_vmem, stats_own, local_sem, r_send, r_recv, z_send, z_recv,
):
    f32, bf16 = jnp.float32, jnp.bfloat16
    rows = query.shape[0]
    chunks = stats.shape[1]
    group = lse_t.shape[0] // (ranges * chunks)
    wide = query.shape[1] // ranges
    narrow = key.shape[1] // ranges
    base, mine, sub = place(ranges)
    g_load = pltpu.make_async_copy(out_grad, g_vmem, local_sem.at[0])
    o_load = pltpu.make_async_copy(output, o_vmem, local_sem.at[1])
    g_load.start()
    o_load.start()
    enter(base, mine, sub, ranges, parts)

    def cut(ref, r, size):
        return ref.at[:, pl.ds(pl.multiple_of(r * size, size), size)]

    def sends(kind, source, target):
        out = []
        for d in range(1, ranges):
            peer = (mine + d) % ranges
            out.append(
                pltpu.make_async_remote_copy(
                    src_ref=source(peer), dst_ref=target,
                    send_sem=r_send.at[kind, d - 1], recv_sem=r_recv.at[kind, d - 1],
                    device_id=(base + peer, sub), device_id_type=MESH,
                )
            )
        own = pltpu.make_async_copy(source(mine), target, local_sem.at[2 + kind])
        for copy in out:
            copy.start()
        own.start()
        return out, own

    k_out, k_own = sends(0, lambda r: cut(key, r, narrow), kv.at[sub, mine, 0])
    v_out, v_own = sends(1, lambda r: cut(value, r, narrow), kv.at[sub, mine, 1])
    q_out, q_own = sends(2, lambda r: cut(query, r, wide), qg.at[mine, 0])
    g_out, g_own = sends(3, lambda r: cut(out_grad, r, wide), qg.at[mine, 1])
    b_out, b_own = sends(4, lambda r: block_keep, keep.at[mine])

    for copy in k_out + v_out:
        copy.wait_recv()
    k_own.wait()
    v_own.wait()
    gathers = []
    for d in range(1, parts):
        copy = pltpu.make_async_remote_copy(
            src_ref=kv.at[sub], dst_ref=kv.at[sub],
            send_sem=z_send.at[d - 1], recv_sem=z_recv.at[d - 1],
            device_id=(base + mine, (sub + d) % parts), device_id_type=MESH,
        )
        copy.start()
        gathers.append(copy)

    g_load.wait()
    o_load.wait()
    ones = jnp.ones((8, 2 * HD), bf16)
    for head in range(lse_t.shape[0]):
        at = slice(head * HD, (head + 1) * HD)
        product = g_vmem[:, at].astype(f32) * o_vmem[:, at].astype(f32)
        high = product.astype(bf16)
        low = (product - high.astype(f32)).astype(bf16)
        both = jnp.concatenate([high, low], axis=1)
        nt = (((1,), (1,)), ((), ()))
        delta = lax.dot_general(ones, both, nt, preferred_element_type=f32)
        r, c, h = head // (chunks * group), head // group % chunks, head % group
        to = slice(h * rows, (h + 1) * rows)
        stats_own[r, c, 0:1, to] = lse_t[head : head + 1, :]
        stats_own[r, c, 1:2, to] = delta[0:1]
    s_out, s_own = sends(5, lambda r: stats_own.at[r], stats.at[mine])

    for copy in k_out + v_out:
        copy.wait_send()
    for copy in gathers + q_out + g_out + b_out + s_out:
        copy.wait()
    for own in (q_own, g_own, b_own, s_own):
        own.wait()


def exchange_in(query, key, value, output, out_grad, lse_t, block_keep, ranges, parts):
    rows, width = query.shape
    heads = lse_t.shape[0]
    chunks = KVH // ranges
    f32, bf16 = jnp.float32, jnp.bfloat16
    anywhere = pl.BlockSpec(memory_space=pl.ANY)
    dma = pltpu.SemaphoreType.DMA
    return pl.pallas_call(
        functools.partial(exchange_in_kernel, ranges, parts),
        out_shape=(
            jax.ShapeDtypeStruct((ranges, 2, rows, width // ranges), bf16),
            jax.ShapeDtypeStruct((ranges, chunks, 2, heads // KVH * rows), f32),
            jax.ShapeDtypeStruct((parts, ranges, 2, rows, key.shape[1] // ranges), bf16),
            jax.ShapeDtypeStruct((ranges,) + block_keep.shape, jnp.int32),
        ),
        in_specs=[anywhere] * 5 + [pl.BlockSpec(memory_space=pltpu.VMEM), anywhere],
        out_specs=(anywhere,) * 4,
        scratch_shapes=[
            pltpu.VMEM((rows, width), bf16),
            pltpu.VMEM((rows, width), bf16),
            pltpu.VMEM((ranges, chunks, 2, heads // KVH * rows), f32),
            dma((8,)),
            dma((6, ranges - 1)),
            dma((6, ranges - 1)),
            dma((parts - 1,)),
            dma((parts - 1,)),
        ],
        compiler_params=pltpu.CompilerParams(
            collective_id=0, has_side_effects=True, vmem_limit_bytes=40 * 1024 * 1024
        ),
    )(query, key, value, output, out_grad, lse_t, block_keep)


def exchange_out_kernel(
    ranges, parts, dq, dkv, query_grad, key_grad, value_grad,
    partial, summed, local_sem, q_send, q_recv, r_send, r_recv, z_send, z_recv,
):
    f32, bf16 = jnp.float32, jnp.bfloat16
    wide = query_grad.shape[1] // ranges
    narrow = key_grad.shape[1] // ranges
    base, mine, sub = place(ranges)
    enter(base, mine, sub, ranges, parts)

    def cut(ref, size):
        return ref.at[:, pl.ds(pl.multiple_of(mine * size, size), size)]

    own = pltpu.make_async_copy(dkv.at[sub], partial.at[sub], local_sem.at[0])
    own.start()
    pieces = []
    for i in range(ranges):
        row = []
        t = i
        for d in range(1, parts):
            peer = (sub + d) % parts
            copy = pltpu.make_async_remote_copy(
                src_ref=dkv.at[peer, t], dst_ref=partial.at[sub, t],
                send_sem=z_send.at[i, d - 1], recv_sem=z_recv.at[i, d - 1],
                device_id=(base + mine, peer), device_id_type=MESH,
            )
            copy.start()
            row.append(copy)
        pieces.append(row)
    out = []
    for d in range(1, ranges):
        peer = (mine + d) % ranges
        copy = pltpu.make_async_remote_copy(
            src_ref=dq.at[peer], dst_ref=cut(query_grad, wide),
            send_sem=q_send.at[d - 1], recv_sem=q_recv.at[d - 1],
            device_id=(base + peer, sub), device_id_type=MESH,
        )
        copy.start()
        out.append(copy)
    q_own = pltpu.make_async_copy(dq.at[mine], cut(query_grad, wide), local_sem.at[1])
    q_own.start()
    own.wait()
    for i in range(ranges):
        for copy in pieces[i]:
            copy.wait_recv()
        for part in range(2):
            total = partial[0, i, part].astype(f32)
            for z in range(1, parts):
                total += partial[z, i, part].astype(f32)
            summed[i, part] = total.astype(bf16)
    owns = []
    for part, grad in enumerate((key_grad, value_grad)):
        for d in range(1, ranges):
            peer = (mine + d) % ranges
            copy = pltpu.make_async_remote_copy(
                src_ref=summed.at[peer, part], dst_ref=cut(grad, narrow),
                send_sem=r_send.at[part, d - 1], recv_sem=r_recv.at[part, d - 1],
                device_id=(base + peer, sub), device_id_type=MESH,
            )
            copy.start()
            out.append(copy)
        grad_own = pltpu.make_async_copy(
            summed.at[mine, part], cut(grad, narrow), local_sem.at[2 + part]
        )
        grad_own.start()
        owns.append(grad_own)
    for row in pieces:
        for copy in row:
            copy.wait_send()
    for copy in out:
        copy.wait()
    q_own.wait()
    for grad_own in owns:
        grad_own.wait()


def exchange_out(dq, dkv, ranges, parts):
    _, rows, wide = dq.shape
    narrow = dkv.shape[-1]
    bf16 = jnp.bfloat16
    anywhere = pl.BlockSpec(memory_space=pl.ANY)
    dma = pltpu.SemaphoreType.DMA
    return pl.pallas_call(
        functools.partial(exchange_out_kernel, ranges, parts),
        out_shape=(
            jax.ShapeDtypeStruct((rows, wide * ranges), bf16),
            jax.ShapeDtypeStruct((rows, narrow * ranges), bf16),
            jax.ShapeDtypeStruct((rows, narrow * ranges), bf16),
        ),
        in_specs=[anywhere] * 2,
        out_specs=(anywhere,) * 3,
        scratch_shapes=[
            pltpu.VMEM(dkv.shape, bf16),
            pltpu.VMEM(dkv.shape[1:], bf16),
            dma((4,)),
            dma((ranges - 1,)),
            dma((ranges - 1,)),
            dma((2, ranges - 1)),
            dma((2, ranges - 1)),
            dma((ranges, parts - 1)),
            dma((ranges, parts - 1)),
        ],
        compiler_params=pltpu.CompilerParams(
            collective_id=1, has_side_effects=True, vmem_limit_bytes=40 * 1024 * 1024
        ),
    )(dq, dkv)


def shards(query, key, value, output, out_grad, lse, doc_lengths, block_keep):
    rows = query.shape[0]
    parts = lax.axis_size("head")
    range_rows = rows * parts
    ranges = DOC_MAX // range_rows
    sub = lax.axis_index("head")
    window = lax.axis_index("blk") // ranges
    starts = (jnp.cumsum(doc_lengths) - doc_lengths - window * DOC_MAX).astype(jnp.int32)
    info = jnp.full((1,), sub * rows, jnp.int32)
    qg, stats, kv, keep = exchange_in(
        query, key, value, output, out_grad, (lse * LOG2E).T, block_keep, ranges, parts
    )
    dq, dkv = attention(info, starts, keep, qg, stats, kv, range_rows)
    return exchange_out(dq, dkv, ranges, parts)


def solution(mesh):
    tokens = P(("blk", "head"), None)
    in_specs = (tokens, tokens, tokens, tokens, tokens, tokens, P(), P("blk", None))
    out_specs = (tokens, tokens, tokens)
    return jax.shard_map(shards, mesh=mesh, in_specs=in_specs, out_specs=out_specs, check_vma=False)
```

```python
import functools
import math

import jax
import jax.numpy as jnp
from jax import lax
from jax.experimental import pallas as pl
from jax.experimental.pallas import tpu as pltpu
from jax.sharding import PartitionSpec as P

KVH = 8
HD = 128
DOC_MAX = 2048
BLOCK = 128
LOG2E = 1.4426950408889634
FAR = 1 << 20
MESH = pl.DeviceIdType.MESH


def place(ranges):
    blk, sub = lax.axis_index("blk"), lax.axis_index("head")
    mine = blk % ranges
    return blk - mine, mine, sub


def enter(base, mine, sub, ranges, parts):
    barrier = pltpu.get_barrier_semaphore()
    for d in range(1, ranges):
        peer = (base + (mine + d) % ranges, sub)
        pl.semaphore_signal(barrier, inc=1, device_id=peer, device_id_type=MESH)
    for d in range(1, parts):
        peer = (base + mine, (sub + d) % parts)
        pl.semaphore_signal(barrier, inc=1, device_id=peer, device_id_type=MESH)
    pl.semaphore_wait(barrier, ranges - 1 + parts - 1)


def whole_kernel(
    ranges, parts, starts, query, key, value, output, out_grad, lse_t, block_keep,
    query_grad, key_grad, value_grad,
    g_vmem, o_vmem, stats_own, stats, qg, kv, keep_in, keep,
    k_all, v_all, kt_all, dk_acc, dv_acc, dqt_acc, dq_out, dkv_out, partial, summed,
    local, r_send, r_recv, z_send, z_recv, q_send, q_recv, p_send, p_recv, f_send, f_recv,
):
    f32, bf16 = jnp.float32, jnp.bfloat16
    rows = query.shape[0]
    chunks = stats.shape[1]
    group = lse_t.shape[0] // (ranges * chunks)
    columns = group * HD
    total = group * rows
    width = min(total, 256)
    span = k_all.shape[0]
    range_rows = rows * parts
    scale = 1.0 / math.sqrt(HD)
    nt = (((1,), (1,)), ((), ()))
    base, mine, sub = place(ranges)
    offset = sub * rows
    keep_row = offset // BLOCK

    g_load = pltpu.make_async_copy(out_grad, g_vmem, local.at[0])
    o_load = pltpu.make_async_copy(output, o_vmem, local.at[1])
    g_load.start()
    o_load.start()
    enter(base, mine, sub, ranges, parts)

    def cut(ref, r, c, size):
        first = pl.multiple_of((r * chunks + c) * size, size)
        return ref.at[:, pl.ds(first, size)]

    def sends(kind, source, target):
        out = []
        for d in range(1, ranges):
            peer = (mine + d) % ranges
            out.append(
                pltpu.make_async_remote_copy(
                    src_ref=source(peer), dst_ref=target,
                    send_sem=r_send.at[kind, d - 1], recv_sem=r_recv.at[kind, d - 1],
                    device_id=(base + peer, sub), device_id_type=MESH,
                )
            )
        own = pltpu.make_async_copy(source(mine), target, local.at[2 + kind])
        for copy in out:
            copy.start()
        own.start()
        return out + [own]

    def kv_sends(c):
        return sends(4 * c, lambda r: cut(key, r, c, HD), kv.at[c, sub, mine, 0]) + sends(
            4 * c + 1, lambda r: cut(value, r, c, HD), kv.at[c, sub, mine, 1]
        )

    def qg_sends(c):
        return sends(4 * c + 2, lambda r: cut(query, r, c, columns), qg.at[c, mine, 0]) + sends(
            4 * c + 3, lambda r: cut(out_grad, r, c, columns), qg.at[c, mine, 1]
        )

    def gather(c):
        out = []
        for d in range(1, parts):
            copy = pltpu.make_async_remote_copy(
                src_ref=kv.at[c, sub], dst_ref=kv.at[c, sub],
                send_sem=z_send.at[c, d - 1], recv_sem=z_recv.at[c, d - 1],
                device_id=(base + mine, (sub + d) % parts), device_id_type=MESH,
            )
            copy.start()
            out.append(copy)
        return out

    def wait(copies):
        for copy in copies:
            copy.wait()

    kv_moves = [kv_sends(c) for c in range(chunks)]
    keep_moves = sends(4 * chunks + 1, lambda r: block_keep, keep_in.at[mine])
    qg_moves = [qg_sends(0)] + [None] * (chunks - 1)
    wait(kv_moves[0])
    gathers = [gather(0)] + [None] * (chunks - 1)

    g_load.wait()
    o_load.wait()
    ones = jnp.ones((8, 2 * HD), bf16)
    for head in range(lse_t.shape[0]):
        at = slice(head * HD, (head + 1) * HD)
        product = g_vmem[:, at].astype(f32) * o_vmem[:, at].astype(f32)
        high = product.astype(bf16)
        low = (product - high.astype(f32)).astype(bf16)
        both = jnp.concatenate([high, low], axis=1)
        delta = lax.dot_general(ones, both, nt, preferred_element_type=f32)
        r, c, h = head // (chunks * group), head // group % chunks, head % group
        to = slice(h * rows, (h + 1) * rows)
        stats_own[r, c, 0:1, to] = lse_t[head : head + 1, :]
        stats_own[r, c, 1:2, to] = delta[0:1]
    stats_moves = sends(4 * chunks, lambda r: stats_own.at[r], stats.at[mine])

    wait(keep_moves)
    keep_copy = pltpu.make_async_copy(keep_in, keep, local.at[0])
    keep_copy.start()
    keep_copy.wait()
    for c in range(1, chunks):
        wait(kv_moves[c])
    wait(stats_moves)

    def doc_start(position):
        found = jnp.zeros_like(position)
        for d in range(starts.shape[0]):
            found = jnp.maximum(found, jnp.where(starts[d] <= position, starts[d], 0))
        return found

    def compute(c, t):
        first_query = t * range_rows + offset
        query_block = first_query // BLOCK
        row_query = first_query + lax.broadcasted_iota(jnp.int32, (1, width), 1) % rows
        row_start = doc_start(row_query)
        heads = range(group)
        queries = [qg[c, t, 0, :, h * HD : (h + 1) * HD] for h in heads]
        grads = [qg[c, t, 1, :, h * HD : (h + 1) * HD] for h in heads]
        queries = jnp.concatenate(queries, axis=0)
        grads = jnp.concatenate(grads, axis=0)
        dqt_acc[...] = jnp.zeros_like(dqt_acc)

        def pair(p, _):
            j = 2 * p
            at = pl.ds(pl.multiple_of(j * BLOCK, 2 * BLOCK), 2 * BLOCK)
            keys, values, keys_t = k_all[at, :], v_all[at, :], kt_all[:, at]
            drop0 = (1 - keep[t, keep_row, query_block - j]) * FAR
            drop1 = (1 - keep[t, keep_row, jnp.maximum(query_block - j - 1, 0)]) * FAR
            line = lax.broadcasted_iota(jnp.int32, (2 * BLOCK, width), 0)
            key_pos = line + j * BLOCK + jnp.where(line < BLOCK, drop0, drop1)
            allowed = (key_pos <= row_query) & (key_pos >= row_start)
            probs_all, dscores_all = [], []
            for first in range(0, total, width):
                q = queries[first : first + width]
                g = grads[first : first + width]
                s = lax.dot_general(keys, q, nt, preferred_element_type=f32)
                dp = lax.dot_general(values, g, nt, preferred_element_type=f32)
                lse = stats[t, c, 0:1, first : first + width]
                delta = stats[t, c, 1:2, first : first + width]
                probs = jnp.where(allowed, jnp.exp2(s * (scale * LOG2E) - lse), 0.0)
                dscores = probs * (dp - delta)
                probs_all.append(probs.astype(bf16))
                dscores_all.append(dscores.astype(bf16))
            probs_all = jnp.concatenate(probs_all, axis=1)
            dscores_all = jnp.concatenate(dscores_all, axis=1)
            dv_acc[at, :] += jnp.dot(probs_all, grads, preferred_element_type=f32)
            dk_acc[at, :] += jnp.dot(dscores_all, queries, preferred_element_type=f32)
            dqt_acc[...] += jnp.dot(keys_t, dscores_all, preferred_element_type=f32)
            return 0

        lax.fori_loop(0, (query_block + 2) // 2, pair, 0)
        for first in range(0, total, width):
            dq = (dqt_acc[:, first : first + width] * scale).T.astype(bf16)
            for h in range(width // rows):
                head = first // rows + h
                dq_out[c, t, :, head * HD : (head + 1) * HD] = dq[h * rows : (h + 1) * rows]
        for z in range(parts):
            first = (t * parts + z) * rows
            dkv_out[c, t, z, 0] = (dk_acc[first : first + rows, :] * scale).astype(bf16)
            dkv_out[c, t, z, 1] = dv_acc[first : first + rows, :].astype(bf16)

    def to_range(t, source, ref, c, size, send, recv, own):
        remote = pltpu.make_async_remote_copy(
            src_ref=source, dst_ref=cut(ref, mine, c, size),
            send_sem=send.at[t], recv_sem=recv.at[mine],
            device_id=(base + t, sub), device_id_type=MESH,
        )
        here = pltpu.make_async_copy(source, cut(ref, mine, c, size), own)

        @pl.when(t != mine)
        def _():
            remote.start()

        @pl.when(t == mine)
        def _():
            here.start()

        def finish():
            @pl.when(t != mine)
            def _():
                remote.wait_send()
                pltpu.make_async_remote_copy(
                    src_ref=source, dst_ref=cut(ref, t, c, size),
                    send_sem=send.at[t], recv_sem=recv.at[t],
                    device_id=(base + t, sub), device_id_type=MESH,
                ).wait_recv()

            @pl.when(t == mine)
            def _():
                here.wait()

        return finish

    def send_partial(c, t):
        out = []
        for d in range(1, parts):
            peer = (sub + d) % parts
            copy = pltpu.make_async_remote_copy(
                src_ref=dkv_out.at[c, t, peer], dst_ref=partial.at[c, t, d - 1],
                send_sem=p_send.at[c, t, d - 1], recv_sem=p_recv.at[c, t, d - 1],
                device_id=(base + mine, peer), device_id_type=MESH,
            )
            copy.start()
            out.append(copy)
        return out

    def add_up(c, t):
        for copy in partials[c, t]:
            copy.wait_recv()
        for part in range(2):
            sums = dkv_out[c, t, sub, part].astype(f32)
            for d in range(parts - 1):
                sums += partial[c, t, d, part].astype(f32)
            summed[c, t, part] = sums.astype(bf16)
        for part, ref in enumerate((key_grad, value_grad)):
            finishes.append(
                to_range(
                    t, summed.at[c, t, part], ref, c, HD,
                    f_send.at[c, part], f_recv.at[c, part], local.at[16 + 2 * c + part],
                )
            )

    partials, finishes = {}, []
    order = list(range(ranges - 1, -1, -1))
    for c in range(chunks):
        wait(qg_moves[c])
        wait(gathers[c])
        if c + 1 < chunks:
            qg_moves[c + 1] = qg_sends(c + 1)
            gathers[c + 1] = gather(c + 1)
        for t in range(ranges):
            for z in range(parts):
                first = (t * parts + z) * rows
                k_all[first : first + rows, :] = kv[c, z, t, 0]
                v_all[first : first + rows, :] = kv[c, z, t, 1]
        for first in range(0, span, 256):
            piece = k_all[first : first + 256, :].astype(f32)
            kt_all[:, first : first + 256] = piece.T.astype(bf16)
        dk_acc[...] = jnp.zeros_like(dk_acc)
        dv_acc[...] = jnp.zeros_like(dv_acc)
        for t in order:
            compute(c, t)
            partials[c, t] = send_partial(c, t)
            finishes.append(
                to_range(
                    t, dq_out.at[c, t], query_grad, c, columns,
                    q_send.at[c], q_recv.at[c], local.at[12 + c],
                )
            )
            if c > 0:
                add_up(c - 1, t)
    for t in order:
        add_up(chunks - 1, t)
    for copies in partials.values():
        for copy in copies:
            copy.wait_send()
    for finish in finishes:
        finish()


def shards(query, key, value, output, out_grad, lse, doc_lengths, block_keep):
    rows, wide = query.shape
    narrow = key.shape[1]
    parts = lax.axis_size("head")
    range_rows = rows * parts
    ranges = DOC_MAX // range_rows
    chunks = KVH // ranges
    columns = wide // KVH
    total = columns // HD * rows
    window = lax.axis_index("blk") // ranges
    starts = (jnp.cumsum(doc_lengths) - doc_lengths - window * DOC_MAX).astype(jnp.int32)
    f32, bf16 = jnp.float32, jnp.bfloat16
    anywhere = pl.BlockSpec(memory_space=pl.ANY)
    vmem, dma = pltpu.VMEM, pltpu.SemaphoreType.DMA
    kinds = 4 * chunks + 2
    return pl.pallas_call(
        functools.partial(whole_kernel, ranges, parts),
        out_shape=(
            jax.ShapeDtypeStruct((rows, wide), bf16),
            jax.ShapeDtypeStruct((rows, narrow), bf16),
            jax.ShapeDtypeStruct((rows, narrow), bf16),
        ),
        in_specs=[pl.BlockSpec(memory_space=pltpu.SMEM)]
        + [anywhere] * 5
        + [pl.BlockSpec(memory_space=pltpu.VMEM), anywhere],
        out_specs=(anywhere,) * 3,
        scratch_shapes=[
            vmem((rows, wide), bf16),
            vmem((rows, wide), bf16),
            vmem((ranges, chunks, 2, total), f32),
            vmem((ranges, chunks, 2, total), f32),
            vmem((chunks, ranges, 2, rows, columns), bf16),
            vmem((chunks, parts, ranges, 2, rows, HD), bf16),
            vmem((ranges,) + block_keep.shape, jnp.int32),
            pltpu.SMEM((ranges,) + block_keep.shape, jnp.int32),
            vmem((DOC_MAX, HD), bf16),
            vmem((DOC_MAX, HD), bf16),
            vmem((HD, DOC_MAX), bf16),
            vmem((DOC_MAX, HD), f32),
            vmem((DOC_MAX, HD), f32),
            vmem((HD, total), f32),
            vmem((chunks, ranges, rows, columns), bf16),
            vmem((chunks, ranges, parts, 2, rows, HD), bf16),
            vmem((chunks, ranges, parts - 1, 2, rows, HD), bf16),
            vmem((chunks, ranges, 2, rows, HD), bf16),
            dma((20,)),
            dma((kinds, ranges - 1)),
            dma((kinds, ranges - 1)),
            dma((chunks, parts - 1)),
            dma((chunks, parts - 1)),
            dma((chunks, ranges)),
            dma((chunks, ranges)),
            dma((chunks, ranges, parts - 1)),
            dma((chunks, ranges, parts - 1)),
            dma((chunks, 2, ranges)),
            dma((chunks, 2, ranges)),
        ],
        compiler_params=pltpu.CompilerParams(
            collective_id=0, has_side_effects=True, vmem_limit_bytes=60 * 1024 * 1024
        ),
        cost_estimate=pl.CostEstimate(
            flops=10 * total * DOC_MAX * HD * ranges * chunks // 2,
            bytes_accessed=7 * rows * wide * 2,
            transcendentals=total * DOC_MAX * ranges * chunks // 2,
        ),
    )(starts, query, key, value, output, out_grad, (lse * LOG2E).T, block_keep)


def solution(mesh):
    tokens = P(("blk", "head"), None)
    in_specs = (tokens, tokens, tokens, tokens, tokens, tokens, P(), P("blk", None))
    out_specs = (tokens, tokens, tokens)
    return jax.shard_map(shards, mesh=mesh, in_specs=in_specs, out_specs=out_specs, check_vma=False)
```

```python
import functools
import math

import jax
import jax.numpy as jnp
from jax import lax
from jax.experimental import pallas as pl
from jax.experimental.pallas import tpu as pltpu
from jax.sharding import PartitionSpec as P

KVH = 8
HD = 128
DOC_MAX = 2048
BLOCK = 128
LOG2E = 1.4426950408889634
FAR = 1 << 20
MESH = pl.DeviceIdType.MESH


def place(ranges):
    blk, sub = lax.axis_index("blk"), lax.axis_index("head")
    mine = blk % ranges
    return blk - mine, mine, sub


def enter(base, mine, sub, ranges, parts):
    barrier = pltpu.get_barrier_semaphore()
    for d in range(1, ranges):
        peer = (base + (mine + d) % ranges, sub)
        pl.semaphore_signal(barrier, inc=1, device_id=peer, device_id_type=MESH)
    for d in range(1, parts):
        peer = (base + mine, (sub + d) % parts)
        pl.semaphore_signal(barrier, inc=1, device_id=peer, device_id_type=MESH)
    pl.semaphore_wait(barrier, ranges - 1 + parts - 1)


def whole_kernel(
    ranges, parts, starts, query, key, value, output, out_grad, lse_t, block_keep,
    query_grad, key_grad, value_grad,
    g_vmem, o_vmem, stats_own, stats, qg, kv, keep_in, keep,
    k_all, v_all, kt_all, dk_acc, dv_acc, dqt_acc, dq_out, dkv_out, partial, summed,
    local, r_send, r_recv, z_send, z_recv, q_send, q_recv, p_send, p_recv, f_send, f_recv,
    relayed, relay_send, relay_recv, q_own, f_own,
):
    f32, bf16 = jnp.float32, jnp.bfloat16
    rows = query.shape[0]
    chunks = kv.shape[0]
    units = stats.shape[1]
    halves = units // chunks
    group = lse_t.shape[0] // (ranges * units)
    relay = parts == 4
    columns = group * HD
    total = group * rows
    width = min(total, 256)
    span = k_all.shape[0]
    range_rows = rows * parts
    scale = 1.0 / math.sqrt(HD)
    nt = (((1,), (1,)), ((), ()))
    base, mine, sub = place(ranges)
    offset = sub * rows
    keep_row = offset // BLOCK

    g_load = pltpu.make_async_copy(out_grad, g_vmem, local.at[0])
    o_load = pltpu.make_async_copy(output, o_vmem, local.at[1])
    g_load.start()
    o_load.start()
    enter(base, mine, sub, ranges, parts)

    def cut(ref, r, c, size):
        first = pl.multiple_of(r * (ref.shape[1] // ranges) + c * size, size)
        return ref.at[:, pl.ds(first, size)]

    def sends(kind, source, target):
        out = []
        for d in range(1, ranges):
            peer = (mine + d) % ranges
            out.append(
                pltpu.make_async_remote_copy(
                    src_ref=source(peer), dst_ref=target,
                    send_sem=r_send.at[kind, d - 1], recv_sem=r_recv.at[kind, d - 1],
                    device_id=(base + peer, sub), device_id_type=MESH,
                )
            )
        own = pltpu.make_async_copy(source(mine), target, local.at[2 + kind])
        for copy in out:
            copy.start()
        own.start()
        return out + [own]

    def kv_sends(c):
        return sends(2 * c, lambda r: cut(key, r, c, HD), kv.at[c, sub, mine, 0]) + sends(
            2 * c + 1, lambda r: cut(value, r, c, HD), kv.at[c, sub, mine, 1]
        )

    def qg_sends(u):
        kind = 2 * chunks + 2 * u
        return sends(kind, lambda r: cut(query, r, u, columns), qg.at[u, mine, 0]) + sends(
            kind + 1, lambda r: cut(out_grad, r, u, columns), qg.at[u, mine, 1]
        )

    def z_copy(src, dst, send, recv, z):
        return pltpu.make_async_remote_copy(
            src_ref=src, dst_ref=dst, send_sem=send, recv_sem=recv,
            device_id=(base + mine, z), device_id_type=MESH,
        )

    def gather_copy(c, z, d, to, whole):
        ref = kv.at[c, z] if whole else kv.at[c, z, pl.ds(0, ranges - 1)]
        return z_copy(ref, ref, z_send.at[c, d - 1], z_recv.at[c, d - 1], to)

    def forward_copy(c):
        return z_copy(kv.at[c, 0], kv.at[c, 0], relay_send.at[c], z_recv.at[c, parts - 2], 3)

    def gather(c):
        for d in range(1, parts):
            peer = (sub + d) % parts
            far = relay and d == parts - 1

            @pl.when((peer > sub) & (not far))
            def _():
                gather_copy(c, sub, d, peer, True).start()

            @pl.when(peer < sub)
            def _():
                gather_copy(c, sub, d, peer, False).start()

    def forward(c):
        if relay:

            @pl.when(sub == 2)
            def _():
                gather_copy(c, 0, 2, 3, True).wait_recv()
                forward_copy(c).start()

    def gathered(c):
        for d in range(1, parts):
            peer = (sub + d) % parts
            origin = (sub - d + parts) % parts
            far = relay and d == parts - 1
            done = (sub == 2) & (relay and d == 2)

            @pl.when((peer > sub) & (not far))
            def _():
                gather_copy(c, sub, d, peer, True).wait_send()

            @pl.when(peer < sub)
            def _():
                gather_copy(c, sub, d, peer, False).wait_send()

            @pl.when((origin < sub) & jnp.logical_not(done))
            def _():
                gather_copy(c, origin, d, peer, True).wait_recv()

            @pl.when(origin > sub)
            def _():
                gather_copy(c, origin, d, peer, False).wait_recv()

        if relay:

            @pl.when(sub == 2)
            def _():
                forward_copy(c).wait_send()

    def wait(copies):
        for copy in copies:
            copy.wait()

    kv_moves = [kv_sends(c) for c in range(chunks)]
    keep_moves = sends(2 * chunks + 2 * units + 1, lambda r: block_keep, keep_in.at[mine])
    qg_moves = [qg_sends(0)] + [None] * (units - 1)
    wait(kv_moves[0])
    gather(0)
    for c in range(chunks):
        for z in range(1, parts):

            @pl.when(z > sub)
            def _():
                kv[c, z, ranges - 1] = jnp.zeros(kv.shape[3:], bf16)

        for d in range(1, parts):
            origin = (sub - d + parts) % parts

            @pl.when(origin < sub)
            def _():
                partial[c, ranges - 1, d - 1] = jnp.zeros(partial.shape[3:], bf16)

        if relay:

            @pl.when(sub == 0)
            def _():
                partial[c, :, 0] = jnp.zeros((ranges,) + partial.shape[3:], bf16)


    g_load.wait()
    o_load.wait()
    ones = jnp.ones((8, 2 * HD), bf16)
    for head in range(lse_t.shape[0]):
        at = slice(head * HD, (head + 1) * HD)
        product = g_vmem[:, at].astype(f32) * o_vmem[:, at].astype(f32)
        high = product.astype(bf16)
        low = (product - high.astype(f32)).astype(bf16)
        both = jnp.concatenate([high, low], axis=1)
        delta = lax.dot_general(ones, both, nt, preferred_element_type=f32)
        r, c, h = head // (units * group), head // group % units, head % group
        to = slice(h * rows, (h + 1) * rows)
        stats_own[r, c, 0:1, to] = lse_t[head : head + 1, :]
        stats_own[r, c, 1:2, to] = delta[0:1]
    stats_moves = sends(2 * chunks + 2 * units, lambda r: stats_own.at[r], stats.at[mine])

    qg_moves[1] = qg_sends(1)
    forward(0)
    wait(keep_moves)
    keep_copy = pltpu.make_async_copy(keep_in, keep, local.at[0])
    keep_copy.start()
    keep_copy.wait()
    for c in range(1, chunks):
        wait(kv_moves[c])
    wait(stats_moves)

    def doc_start(position):
        found = jnp.zeros_like(position)
        for d in range(starts.shape[0]):
            found = jnp.maximum(found, jnp.where(starts[d] <= position, starts[d], 0))
        return found

    def compute(u, t):
        first_query = t * range_rows + offset
        query_block = first_query // BLOCK
        row_query = first_query + lax.broadcasted_iota(jnp.int32, (1, width), 1) % rows
        row_start = doc_start(row_query)
        heads = range(group)
        queries = [qg[u, t, 0, :, h * HD : (h + 1) * HD] for h in heads]
        grads = [qg[u, t, 1, :, h * HD : (h + 1) * HD] for h in heads]
        queries = jnp.concatenate(queries, axis=0)
        grads = jnp.concatenate(grads, axis=0)
        dqt_acc[...] = jnp.zeros_like(dqt_acc)

        def pair(p, _):
            j = 2 * p
            at = pl.ds(pl.multiple_of(j * BLOCK, 2 * BLOCK), 2 * BLOCK)
            keys, values, keys_t = k_all[at, :], v_all[at, :], kt_all[:, at]
            drop0 = (1 - keep[t, keep_row, query_block - j]) * FAR
            drop1 = (1 - keep[t, keep_row, jnp.maximum(query_block - j - 1, 0)]) * FAR
            line = lax.broadcasted_iota(jnp.int32, (2 * BLOCK, width), 0)
            key_pos = line + j * BLOCK + jnp.where(line < BLOCK, drop0, drop1)
            allowed = (key_pos <= row_query) & (key_pos >= row_start)
            probs_all, dscores_all = [], []
            for first in range(0, total, width):
                q = queries[first : first + width]
                g = grads[first : first + width]
                s = lax.dot_general(keys, q, nt, preferred_element_type=f32)
                dp = lax.dot_general(values, g, nt, preferred_element_type=f32)
                lse = stats[t, u, 0:1, first : first + width]
                delta = stats[t, u, 1:2, first : first + width]
                probs = jnp.where(allowed, jnp.exp2(s * (scale * LOG2E) - lse), 0.0)
                dscores = probs * (dp - delta)
                probs_all.append(probs.astype(bf16))
                dscores_all.append(dscores.astype(bf16))
            probs_all = jnp.concatenate(probs_all, axis=1)
            dscores_all = jnp.concatenate(dscores_all, axis=1)
            dv_acc[at, :] += jnp.dot(probs_all, grads, preferred_element_type=f32)
            dk_acc[at, :] += jnp.dot(dscores_all, queries, preferred_element_type=f32)
            dqt_acc[...] += jnp.dot(keys_t, dscores_all, preferred_element_type=f32)
            return 0

        lax.fori_loop(0, (query_block + 2) // 2, pair, 0)
        for first in range(0, total, width):
            dq = (dqt_acc[:, first : first + width] * scale).T.astype(bf16)
            for h in range(width // rows):
                head = first // rows + h
                dq_out[u, t, :, head * HD : (head + 1) * HD] = dq[h * rows : (h + 1) * rows]

    def store(c, t):
        for z in range(parts):
            first = (t * parts + z) * rows
            dkv_out[c, t, z, 0] = (dk_acc[first : first + rows, :] * scale).astype(bf16)
            dkv_out[c, t, z, 1] = dv_acc[first : first + rows, :].astype(bf16)

    def to_range(t, source, ref, c, size, send, recv, own):
        remote = pltpu.make_async_remote_copy(
            src_ref=source, dst_ref=cut(ref, mine, c, size),
            send_sem=send.at[t], recv_sem=recv.at[mine],
            device_id=(base + t, sub), device_id_type=MESH,
        )
        here = pltpu.make_async_copy(source, cut(ref, mine, c, size), own)

        @pl.when(t != mine)
        def _():
            remote.start()

        @pl.when(t == mine)
        def _():
            here.start()

        def finish():
            @pl.when(t != mine)
            def _():
                remote.wait_send()
                pltpu.make_async_remote_copy(
                    src_ref=source, dst_ref=cut(ref, t, c, size),
                    send_sem=send.at[t], recv_sem=recv.at[t],
                    device_id=(base + t, sub), device_id_type=MESH,
                ).wait_recv()

            @pl.when(t == mine)
            def _():
                here.wait()

        return finish

    def partial_copy(c, t, d, peer):
        return z_copy(
            dkv_out.at[c, t, peer], partial.at[c, t, d - 1],
            p_send.at[c, t, d - 1], p_recv.at[c, t, d - 1], peer,
        )

    def far_copy(c, t):
        return z_copy(
            dkv_out.at[c, t, 0], relayed.at[c, t],
            p_send.at[c, t, 0], relay_recv.at[c, t], 2,
        )

    def is_sent(t, d, peer, origin):
        sent = (peer < origin) | (t < ranges - 1)
        if relay and d == 1:
            sent = sent & (origin != 3)
        return sent

    def send_partial(c, t):
        for d in range(1, parts):
            peer = (sub + d) % parts
            late = (sub == 2) & (relay and d == 2)

            @pl.when(is_sent(t, d, peer, sub) & jnp.logical_not(late))
            def _():
                partial_copy(c, t, d, peer).start()

        if relay:

            @pl.when(sub == 3)
            def _():
                far_copy(c, t).start()

    def send_late(c, t):
        if relay:

            @pl.when(sub == 2)
            def _():
                far_copy(c, t).wait_recv()
                both = dkv_out[c, t, 0].astype(f32) + relayed[c, t].astype(f32)
                dkv_out[c, t, 0] = both.astype(bf16)
                partial_copy(c, t, 2, 0).start()

    def sent_partial(c, t):
        for d in range(1, parts):
            peer = (sub + d) % parts

            @pl.when(is_sent(t, d, peer, sub))
            def _():
                partial_copy(c, t, d, peer).wait_send()

        if relay:

            @pl.when(sub == 3)
            def _():
                far_copy(c, t).wait_send()

    def add_up(c, t):
        for d in range(1, parts):
            origin = (sub - d + parts) % parts

            @pl.when(is_sent(t, d, sub, origin))
            def _():
                partial_copy(c, t, d, (sub + d) % parts).wait_recv()

        for part in range(2):
            sums = dkv_out[c, t, sub, part].astype(f32)
            for d in range(parts - 1):
                sums += partial[c, t, d, part].astype(f32)
            summed[c, t, part] = sums.astype(bf16)
        for part, ref in enumerate((key_grad, value_grad)):
            finishes.append(
                to_range(
                    t, summed.at[c, t, part], ref, c, HD,
                    f_send.at[c, part], f_recv.at[c, part], f_own.at[c, part],
                )
            )

    finishes = []
    order = list(range(ranges - 1, -1, -1))
    late, ready = [], []
    for u in range(units):
        c = u // halves
        wait(qg_moves[u])
        if u % halves == 0:
            gathered(c)
            if c + 1 < chunks:
                gather(c + 1)
            for t in range(ranges):
                for z in range(parts):
                    first = (t * parts + z) * rows
                    k_all[first : first + rows, :] = kv[c, z, t, 0]
                    v_all[first : first + rows, :] = kv[c, z, t, 1]
            for first in range(0, span, 256):
                piece = k_all[first : first + 256, :].astype(f32)
                kt_all[:, first : first + 256] = piece.T.astype(bf16)
            dk_acc[...] = jnp.zeros_like(dk_acc)
            dv_acc[...] = jnp.zeros_like(dv_acc)
        for i, t in enumerate(order):
            compute(u, t)
            finishes.append(
                to_range(
                    t, dq_out.at[u, t], query_grad, u, columns,
                    q_send.at[u], q_recv.at[u], q_own.at[u],
                )
            )
            if late:
                at = late.pop(0)
                send_late(*at)
                ready.append(at)
            if len(ready) > 3 or (ready and u % halves == 0):
                add_up(*ready.pop(0))
            if u % halves == halves - 1:
                store(c, t)
                send_partial(c, t)
                late.append((c, t))
            if i == 1 and u + 2 < units:
                qg_moves[u + 2] = qg_sends(u + 2)
            if i == ranges - 1 and u % halves == 0 and c + 1 < chunks:
                forward(c + 1)
    for at in late:
        send_late(*at)
        ready.append(at)
    for at in ready:
        add_up(*at)
    for c in range(chunks):
        for t in order:
            sent_partial(c, t)
    for finish in finishes:
        finish()


def shards(query, key, value, output, out_grad, lse, doc_lengths, block_keep):
    rows, wide = query.shape
    narrow = key.shape[1]
    parts = lax.axis_size("head")
    range_rows = rows * parts
    ranges = DOC_MAX // range_rows
    chunks = KVH // ranges
    units = 2 * chunks
    columns = wide // (ranges * units)
    total = columns // HD * rows
    window = lax.axis_index("blk") // ranges
    starts = (jnp.cumsum(doc_lengths) - doc_lengths - window * DOC_MAX).astype(jnp.int32)
    f32, bf16 = jnp.float32, jnp.bfloat16
    anywhere = pl.BlockSpec(memory_space=pl.ANY)
    vmem, dma = pltpu.VMEM, pltpu.SemaphoreType.DMA
    kinds = 2 * chunks + 2 * units + 2
    return pl.pallas_call(
        functools.partial(whole_kernel, ranges, parts),
        out_shape=(
            jax.ShapeDtypeStruct((rows, wide), bf16),
            jax.ShapeDtypeStruct((rows, narrow), bf16),
            jax.ShapeDtypeStruct((rows, narrow), bf16),
        ),
        in_specs=[pl.BlockSpec(memory_space=pltpu.SMEM)]
        + [anywhere] * 5
        + [pl.BlockSpec(memory_space=pltpu.VMEM), anywhere],
        out_specs=(anywhere,) * 3,
        scratch_shapes=[
            vmem((rows, wide), bf16),
            vmem((rows, wide), bf16),
            vmem((ranges, units, 2, total), f32),
            vmem((ranges, units, 2, total), f32),
            vmem((units, ranges, 2, rows, columns), bf16),
            vmem((chunks, parts, ranges, 2, rows, HD), bf16),
            vmem((ranges,) + block_keep.shape, jnp.int32),
            pltpu.SMEM((ranges,) + block_keep.shape, jnp.int32),
            vmem((DOC_MAX, HD), bf16),
            vmem((DOC_MAX, HD), bf16),
            vmem((HD, DOC_MAX), bf16),
            vmem((DOC_MAX, HD), f32),
            vmem((DOC_MAX, HD), f32),
            vmem((HD, total), f32),
            vmem((units, ranges, rows, columns), bf16),
            vmem((chunks, ranges, parts, 2, rows, HD), bf16),
            vmem((chunks, ranges, parts - 1, 2, rows, HD), bf16),
            vmem((chunks, ranges, 2, rows, HD), bf16),
            dma((2 + kinds,)),
            dma((kinds, ranges - 1)),
            dma((kinds, ranges - 1)),
            dma((chunks, parts - 1)),
            dma((chunks, parts - 1)),
            dma((units, ranges)),
            dma((units, ranges)),
            dma((chunks, ranges, parts - 1)),
            dma((chunks, ranges, parts - 1)),
            dma((chunks, 2, ranges)),
            dma((chunks, 2, ranges)),
            vmem((chunks, ranges, 2, rows, HD), bf16),
            dma((chunks,)),
            dma((chunks, ranges)),
            dma((units,)),
            dma((chunks, 2)),
        ],
        compiler_params=pltpu.CompilerParams(
            collective_id=0, has_side_effects=True, vmem_limit_bytes=60 * 1024 * 1024
        ),
        cost_estimate=pl.CostEstimate(
            flops=10 * total * DOC_MAX * HD * ranges * chunks // 2,
            bytes_accessed=7 * rows * wide * 2,
            transcendentals=total * DOC_MAX * ranges * chunks // 2,
        ),
    )(starts, query, key, value, output, out_grad, (lse * LOG2E).T, block_keep)


def solution(mesh):
    tokens = P(("blk", "head"), None)
    in_specs = (tokens, tokens, tokens, tokens, tokens, tokens, P(), P("blk", None))
    out_specs = (tokens, tokens, tokens)
    return jax.shard_map(shards, mesh=mesh, in_specs=in_specs, out_specs=out_specs, check_vma=False)
```

```python
import functools
import math

import jax
import jax.numpy as jnp
from jax import lax
from jax.experimental import pallas as pl
from jax.experimental.pallas import tpu as pltpu
from jax.sharding import PartitionSpec as P

KVH = 8
HD = 128
DOC_MAX = 2048
BLOCK = 128
LOG2E = 1.4426950408889634
FAR = 1 << 20
MESH = pl.DeviceIdType.MESH


def place(ranges):
    blk, sub = lax.axis_index("blk"), lax.axis_index("head")
    mine = blk % ranges
    return blk - mine, mine, sub


def enter(base, mine, sub, ranges, parts):
    barrier = pltpu.get_barrier_semaphore()
    for d in range(1, ranges):
        peer = (base + (mine + d) % ranges, sub)
        pl.semaphore_signal(barrier, inc=1, device_id=peer, device_id_type=MESH)
    for d in range(1, parts):
        peer = (base + mine, (sub + d) % parts)
        pl.semaphore_signal(barrier, inc=1, device_id=peer, device_id_type=MESH)
    pl.semaphore_wait(barrier, ranges - 1 + parts - 1)


def whole_kernel(
    ranges, parts, lengths, query, key, value, output, out_grad, lse_t, block_keep,
    query_grad, key_grad, value_grad,
    g_vmem, o_vmem, stats_own, stats, qg, kv, keep_in, keep,
    k_all, v_all, kt_all, dk_acc, dv_acc, dqt_acc, dq_out, dkv_out, partial, summed,
    local, r_send, r_recv, z_send, z_recv, q_send, q_recv, p_send, p_recv, f_send, f_recv,
    relayed, relay_send, relay_recv, q_own, f_own,
):
    f32, bf16 = jnp.float32, jnp.bfloat16
    rows = query.shape[0]
    chunks = kv.shape[0]
    units = stats.shape[1]
    halves = units // chunks
    group = lse_t.shape[0] // (ranges * units)
    relay = parts == 4
    columns = group * HD
    total = group * rows
    width = min(total, 256)
    span = k_all.shape[0]
    range_rows = rows * parts
    scale = 1.0 / math.sqrt(HD)
    nt = (((1,), (1,)), ((), ()))
    base, mine, sub = place(ranges)
    offset = sub * rows
    keep_row = offset // BLOCK

    g_load = pltpu.make_async_copy(out_grad, g_vmem, local.at[0])
    o_load = pltpu.make_async_copy(output, o_vmem, local.at[1])
    g_load.start()
    o_load.start()
    enter(base, mine, sub, ranges, parts)

    def cut(ref, r, c, size):
        first = pl.multiple_of(r * (ref.shape[1] // ranges) + c * size, size)
        return ref.at[:, pl.ds(first, size)]

    def sends(kind, source, target):
        out = []
        for d in range(1, ranges):
            peer = (mine + d) % ranges
            out.append(
                pltpu.make_async_remote_copy(
                    src_ref=source(peer), dst_ref=target,
                    send_sem=r_send.at[kind, d - 1], recv_sem=r_recv.at[kind, d - 1],
                    device_id=(base + peer, sub), device_id_type=MESH,
                )
            )
        own = pltpu.make_async_copy(source(mine), target, local.at[2 + kind])
        for copy in out:
            copy.start()
        own.start()
        return out + [own]

    def kv_sends(c):
        return sends(2 * c, lambda r: cut(key, r, c, HD), kv.at[c, sub, mine, 0]) + sends(
            2 * c + 1, lambda r: cut(value, r, c, HD), kv.at[c, sub, mine, 1]
        )

    def qg_sends(u):
        kind = 2 * chunks + 2 * u
        return sends(kind, lambda r: cut(query, r, u, columns), qg.at[u, mine, 0]) + sends(
            kind + 1, lambda r: cut(out_grad, r, u, columns), qg.at[u, mine, 1]
        )

    def z_copy(src, dst, send, recv, z):
        return pltpu.make_async_remote_copy(
            src_ref=src, dst_ref=dst, send_sem=send, recv_sem=recv,
            device_id=(base + mine, z), device_id_type=MESH,
        )

    def gather_copy(c, z, d, to, whole):
        ref = kv.at[c, z] if whole else kv.at[c, z, pl.ds(0, ranges - 1)]
        return z_copy(ref, ref, z_send.at[c, d - 1], z_recv.at[c, d - 1], to)

    def forward_copy(c):
        return z_copy(kv.at[c, 0], kv.at[c, 0], relay_send.at[c], z_recv.at[c, parts - 2], 3)

    def gather(c):
        for d in range(1, parts):
            peer = (sub + d) % parts
            far = relay and d == parts - 1

            @pl.when((peer > sub) & (not far))
            def _():
                gather_copy(c, sub, d, peer, True).start()

            @pl.when(peer < sub)
            def _():
                gather_copy(c, sub, d, peer, False).start()

    def forward(c):
        if relay:

            @pl.when(sub == 2)
            def _():
                gather_copy(c, 0, 2, 3, True).wait_recv()
                forward_copy(c).start()

    def gathered(c):
        for d in range(1, parts):
            peer = (sub + d) % parts
            origin = (sub - d + parts) % parts
            far = relay and d == parts - 1
            done = (sub == 2) & (relay and d == 2)

            @pl.when((peer > sub) & (not far))
            def _():
                gather_copy(c, sub, d, peer, True).wait_send()

            @pl.when(peer < sub)
            def _():
                gather_copy(c, sub, d, peer, False).wait_send()

            @pl.when((origin < sub) & jnp.logical_not(done))
            def _():
                gather_copy(c, origin, d, peer, True).wait_recv()

            @pl.when(origin > sub)
            def _():
                gather_copy(c, origin, d, peer, False).wait_recv()

        if relay:

            @pl.when(sub == 2)
            def _():
                forward_copy(c).wait_send()

    def wait(copies):
        for copy in copies:
            copy.wait()

    kv_moves = [kv_sends(c) for c in range(chunks)]
    keep_moves = sends(2 * chunks + 2 * units + 1, lambda r: block_keep, keep_in.at[mine])
    qg_moves = [qg_sends(0)] + [None] * (units - 1)
    wait(kv_moves[0])
    gather(0)
    for c in range(chunks):
        for z in range(1, parts):

            @pl.when(z > sub)
            def _():
                kv[c, z, ranges - 1] = jnp.zeros(kv.shape[3:], bf16)

        for d in range(1, parts):
            origin = (sub - d + parts) % parts

            @pl.when(origin < sub)
            def _():
                partial[c, ranges - 1, d - 1] = jnp.zeros(partial.shape[3:], bf16)

        if relay:

            @pl.when(sub == 0)
            def _():
                partial[c, :, 0] = jnp.zeros((ranges,) + partial.shape[3:], bf16)


    g_load.wait()
    o_load.wait()
    ones = jnp.ones((8, 2 * HD), bf16)
    for head in range(lse_t.shape[0]):
        at = slice(head * HD, (head + 1) * HD)
        product = g_vmem[:, at].astype(f32) * o_vmem[:, at].astype(f32)
        high = product.astype(bf16)
        low = (product - high.astype(f32)).astype(bf16)
        both = jnp.concatenate([high, low], axis=1)
        delta = lax.dot_general(ones, both, nt, preferred_element_type=f32)
        r, c, h = head // (units * group), head // group % units, head % group
        to = slice(h * rows, (h + 1) * rows)
        stats_own[r, c, 0:1, to] = lse_t[head : head + 1, :]
        stats_own[r, c, 1:2, to] = delta[0:1]
    stats_moves = sends(2 * chunks + 2 * units, lambda r: stats_own.at[r], stats.at[mine])

    forward(0)
    wait(keep_moves)
    keep_copy = pltpu.make_async_copy(keep_in, keep, local.at[0])
    keep_copy.start()
    keep_copy.wait()
    for c in range(1, chunks):
        wait(kv_moves[c])
    wait(stats_moves)

    def doc_start(position):
        found = jnp.zeros_like(position)
        start = -(base // ranges) * DOC_MAX
        for d in range(lengths.shape[0]):
            found = jnp.maximum(found, jnp.where(start <= position, start, 0))
            start = start + lengths[d]
        return found

    def compute(u, t):
        first_query = t * range_rows + offset
        query_block = first_query // BLOCK
        row_query = first_query + lax.broadcasted_iota(jnp.int32, (1, width), 1) % rows
        row_start = doc_start(row_query)
        heads = range(group)
        queries = [qg[u, t, 0, :, h * HD : (h + 1) * HD] for h in heads]
        grads = [qg[u, t, 1, :, h * HD : (h + 1) * HD] for h in heads]
        queries = jnp.concatenate(queries, axis=0)
        grads = jnp.concatenate(grads, axis=0)
        dqt_acc[...] = jnp.zeros_like(dqt_acc)

        def pair(p, _):
            j = 2 * p
            at = pl.ds(pl.multiple_of(j * BLOCK, 2 * BLOCK), 2 * BLOCK)
            keys, values, keys_t = k_all[at, :], v_all[at, :], kt_all[:, at]
            drop0 = (1 - keep[t, keep_row, query_block - j]) * FAR
            drop1 = (1 - keep[t, keep_row, jnp.maximum(query_block - j - 1, 0)]) * FAR
            line = lax.broadcasted_iota(jnp.int32, (2 * BLOCK, width), 0)
            key_pos = line + j * BLOCK + jnp.where(line < BLOCK, drop0, drop1)
            allowed = (key_pos <= row_query) & (key_pos >= row_start)
            probs_all, dscores_all = [], []
            for first in range(0, total, width):
                q = queries[first : first + width]
                g = grads[first : first + width]
                s = lax.dot_general(keys, q, nt, preferred_element_type=f32)
                dp = lax.dot_general(values, g, nt, preferred_element_type=f32)
                lse = stats[t, u, 0:1, first : first + width]
                delta = stats[t, u, 1:2, first : first + width]
                probs = jnp.where(allowed, jnp.exp2(s * (scale * LOG2E) - lse), 0.0)
                dscores = probs * (dp - delta)
                probs_all.append(probs.astype(bf16))
                dscores_all.append(dscores.astype(bf16))
            probs_all = jnp.concatenate(probs_all, axis=1)
            dscores_all = jnp.concatenate(dscores_all, axis=1)
            dv_acc[at, :] += jnp.dot(probs_all, grads, preferred_element_type=f32)
            dk_acc[at, :] += jnp.dot(dscores_all, queries, preferred_element_type=f32)
            dqt_acc[...] += jnp.dot(keys_t, dscores_all, preferred_element_type=f32)
            return 0

        lax.fori_loop(0, (query_block + 2) // 2, pair, 0)
        for first in range(0, total, width):
            dq = (dqt_acc[:, first : first + width] * scale).T.astype(bf16)
            for h in range(width // rows):
                head = first // rows + h
                dq_out[u, t, :, head * HD : (head + 1) * HD] = dq[h * rows : (h + 1) * rows]

    def store(c, t):
        for z in range(parts):
            first = (t * parts + z) * rows
            dkv_out[c, t, z, 0] = (dk_acc[first : first + rows, :] * scale).astype(bf16)
            dkv_out[c, t, z, 1] = dv_acc[first : first + rows, :].astype(bf16)

    def to_range(t, source, ref, c, size, send, recv, own):
        remote = pltpu.make_async_remote_copy(
            src_ref=source, dst_ref=cut(ref, mine, c, size),
            send_sem=send.at[t], recv_sem=recv.at[mine],
            device_id=(base + t, sub), device_id_type=MESH,
        )
        here = pltpu.make_async_copy(source, cut(ref, mine, c, size), own)

        @pl.when(t != mine)
        def _():
            remote.start()

        @pl.when(t == mine)
        def _():
            here.start()

        def finish():
            @pl.when(t != mine)
            def _():
                remote.wait_send()
                pltpu.make_async_remote_copy(
                    src_ref=source, dst_ref=cut(ref, t, c, size),
                    send_sem=send.at[t], recv_sem=recv.at[t],
                    device_id=(base + t, sub), device_id_type=MESH,
                ).wait_recv()

            @pl.when(t == mine)
            def _():
                here.wait()

        return finish

    def partial_copy(c, t, d, peer):
        return z_copy(
            dkv_out.at[c, t, peer], partial.at[c, t, d - 1],
            p_send.at[c, t, d - 1], p_recv.at[c, t, d - 1], peer,
        )

    def far_copy(c, t):
        return z_copy(
            dkv_out.at[c, t, 0], relayed.at[c, t],
            p_send.at[c, t, 0], relay_recv.at[c, t], 2,
        )

    def is_sent(t, d, peer, origin):
        sent = (peer < origin) | (t < ranges - 1)
        if relay and d == 1:
            sent = sent & (origin != 3)
        return sent

    def send_partial(c, t):
        for d in range(1, parts):
            peer = (sub + d) % parts
            late = (sub == 2) & (relay and d == 2)

            @pl.when(is_sent(t, d, peer, sub) & jnp.logical_not(late))
            def _():
                partial_copy(c, t, d, peer).start()

        if relay:

            @pl.when(sub == 3)
            def _():
                far_copy(c, t).start()

    def send_late(c, t):
        if relay:

            @pl.when(sub == 2)
            def _():
                far_copy(c, t).wait_recv()
                both = dkv_out[c, t, 0].astype(f32) + relayed[c, t].astype(f32)
                dkv_out[c, t, 0] = both.astype(bf16)
                partial_copy(c, t, 2, 0).start()

    def sent_partial(c, t):
        for d in range(1, parts):
            peer = (sub + d) % parts

            @pl.when(is_sent(t, d, peer, sub))
            def _():
                partial_copy(c, t, d, peer).wait_send()

        if relay:

            @pl.when(sub == 3)
            def _():
                far_copy(c, t).wait_send()

    def add_up(c, t):
        for d in range(1, parts):
            origin = (sub - d + parts) % parts

            @pl.when(is_sent(t, d, sub, origin))
            def _():
                partial_copy(c, t, d, (sub + d) % parts).wait_recv()

        for part in range(2):
            sums = dkv_out[c, t, sub, part].astype(f32)
            for d in range(parts - 1):
                sums += partial[c, t, d, part].astype(f32)
            summed[c, t, part] = sums.astype(bf16)
        for part, ref in enumerate((key_grad, value_grad)):
            finishes.append(
                to_range(
                    t, summed.at[c, t, part], ref, c, HD,
                    f_send.at[c, part], f_recv.at[c, part], f_own.at[c, part],
                )
            )

    finishes = []
    order = list(range(ranges - 1, -1, -1))
    late, ready = [], []

    def send_dq(u, t):
        finishes.append(
            to_range(
                t, dq_out.at[u, t], query_grad, u, columns,
                q_send.at[u], q_recv.at[u], q_own.at[u],
            )
        )

    for u in range(units):
        c = u // halves
        wait(qg_moves[u])
        if u + 1 < units:
            qg_moves[u + 1] = qg_sends(u + 1)
        for held in order if u > 0 else ():
            send_dq(u - 1, held)
        if u % halves == 0:
            gathered(c)
            if c + 1 < chunks:
                gather(c + 1)
            for t in range(ranges):
                for z in range(parts):
                    first = (t * parts + z) * rows
                    k_all[first : first + rows, :] = kv[c, z, t, 0]
                    v_all[first : first + rows, :] = kv[c, z, t, 1]
            for first in range(0, span, 256):
                piece = k_all[first : first + 256, :].astype(f32)
                kt_all[:, first : first + 256] = piece.T.astype(bf16)
            dk_acc[...] = jnp.zeros_like(dk_acc)
            dv_acc[...] = jnp.zeros_like(dv_acc)
        for i, t in enumerate(order):
            compute(u, t)
            if u == units - 1:
                send_dq(u, t)
            if u % halves == halves - 1:
                store(c, t)
                send_partial(c, t)
                late.append((c, t))
            if len(late) > 1:
                at = late.pop(0)
                send_late(*at)
                ready.append(at)
            if len(ready) > ranges - 1:
                add_up(*ready.pop(0))
            if i == 1 and u % halves == 0 and c + 1 < chunks:
                forward(c + 1)
    for at in late:
        send_late(*at)
        ready.append(at)
    for at in ready:
        add_up(*at)
    for c in range(chunks):
        for t in order:
            sent_partial(c, t)
    for finish in finishes:
        finish()


def shards(query, key, value, output, out_grad, lse, doc_lengths, block_keep):
    rows, wide = query.shape
    narrow = key.shape[1]
    parts = lax.axis_size("head")
    range_rows = rows * parts
    ranges = DOC_MAX // range_rows
    chunks = KVH // ranges
    units = chunks
    columns = wide // (ranges * units)
    total = columns // HD * rows
    f32, bf16 = jnp.float32, jnp.bfloat16
    anywhere = pl.BlockSpec(memory_space=pl.ANY)
    vmem, dma = pltpu.VMEM, pltpu.SemaphoreType.DMA
    kinds = 2 * chunks + 2 * units + 2
    return pl.pallas_call(
        functools.partial(whole_kernel, ranges, parts),
        out_shape=(
            jax.ShapeDtypeStruct((rows, wide), bf16),
            jax.ShapeDtypeStruct((rows, narrow), bf16),
            jax.ShapeDtypeStruct((rows, narrow), bf16),
        ),
        in_specs=[pl.BlockSpec(memory_space=pltpu.SMEM)]
        + [anywhere] * 5
        + [pl.BlockSpec(memory_space=pltpu.VMEM), anywhere],
        out_specs=(anywhere,) * 3,
        scratch_shapes=[
            vmem((rows, wide), bf16),
            vmem((rows, wide), bf16),
            vmem((ranges, units, 2, total), f32),
            vmem((ranges, units, 2, total), f32),
            vmem((units, ranges, 2, rows, columns), bf16),
            vmem((chunks, parts, ranges, 2, rows, HD), bf16),
            vmem((ranges,) + block_keep.shape, jnp.int32),
            pltpu.SMEM((ranges,) + block_keep.shape, jnp.int32),
            vmem((DOC_MAX, HD), bf16),
            vmem((DOC_MAX, HD), bf16),
            vmem((HD, DOC_MAX), bf16),
            vmem((DOC_MAX, HD), f32),
            vmem((DOC_MAX, HD), f32),
            vmem((HD, total), f32),
            vmem((units, ranges, rows, columns), bf16),
            vmem((chunks, ranges, parts, 2, rows, HD), bf16),
            vmem((chunks, ranges, parts - 1, 2, rows, HD), bf16),
            vmem((chunks, ranges, 2, rows, HD), bf16),
            dma((2 + kinds,)),
            dma((kinds, ranges - 1)),
            dma((kinds, ranges - 1)),
            dma((chunks, parts - 1)),
            dma((chunks, parts - 1)),
            dma((units, ranges)),
            dma((units, ranges)),
            dma((chunks, ranges, parts - 1)),
            dma((chunks, ranges, parts - 1)),
            dma((chunks, 2, ranges)),
            dma((chunks, 2, ranges)),
            vmem((chunks, ranges, 2, rows, HD), bf16),
            dma((chunks,)),
            dma((chunks, ranges)),
            dma((units,)),
            dma((chunks, 2)),
        ],
        compiler_params=pltpu.CompilerParams(
            collective_id=0, has_side_effects=True, vmem_limit_bytes=60 * 1024 * 1024
        ),
        cost_estimate=pl.CostEstimate(
            flops=10 * total * DOC_MAX * HD * ranges * chunks // 2,
            bytes_accessed=7 * rows * wide * 2,
            transcendentals=total * DOC_MAX * ranges * chunks // 2,
        ),
    )(doc_lengths, query, key, value, output, out_grad, (lse * LOG2E).T, block_keep)


def solution(mesh):
    tokens = P(("blk", "head"), None)
    in_specs = (tokens, tokens, tokens, tokens, tokens, tokens, P(), P("blk", None))
    out_specs = (tokens, tokens, tokens)
    return jax.shard_map(shards, mesh=mesh, in_specs=in_specs, out_specs=out_specs, check_vma=False)
```

```python
import functools
import math

import jax
import jax.numpy as jnp
from jax import lax
from jax.experimental import pallas as pl
from jax.experimental.pallas import tpu as pltpu
from jax.sharding import PartitionSpec as P

KVH = 8
HD = 128
DOC_MAX = 2048
BLOCK = 128
LOG2E = 1.4426950408889634
FAR = 1 << 20
MESH = pl.DeviceIdType.MESH


def place(ranges):
    blk, sub = lax.axis_index("blk"), lax.axis_index("head")
    mine = blk % ranges
    return blk - mine, mine, sub


def enter(base, mine, sub, ranges, parts):
    barrier = pltpu.get_barrier_semaphore()
    for d in range(1, ranges):
        peer = (base + (mine + d) % ranges, sub)
        pl.semaphore_signal(barrier, inc=1, device_id=peer, device_id_type=MESH)
    for d in range(1, parts):
        peer = (base + mine, (sub + d) % parts)
        pl.semaphore_signal(barrier, inc=1, device_id=peer, device_id_type=MESH)
    pl.semaphore_wait(barrier, ranges - 1 + parts - 1)


def whole_kernel(
    ranges, parts, lengths, query, key, value, output, out_grad, lse_t, block_keep,
    query_grad, key_grad, value_grad,
    g_vmem, o_vmem, stats_own, stats, qg, kv, keep_in, keep,
    k_all, v_all, kt_all, dk_acc, dv_acc, dqt_acc, dq_out, dkv_out, partial, summed,
    local, r_send, r_recv, z_send, z_recv, q_send, q_recv, p_send, p_recv, f_send, f_recv,
    relayed, relay_send, relay_recv, q_own, f_own,
):
    f32, bf16 = jnp.float32, jnp.bfloat16
    rows = query.shape[0]
    chunks = kv.shape[0]
    units = stats.shape[1]
    halves = units // chunks
    group = lse_t.shape[0] // (ranges * units)
    relay = parts == 4
    columns = group * HD
    total = group * rows
    width = min(total, 256)
    span = k_all.shape[0]
    range_rows = rows * parts
    scale = 1.0 / math.sqrt(HD)
    nt = (((1,), (1,)), ((), ()))
    base, mine, sub = place(ranges)
    offset = sub * rows
    keep_row = offset // BLOCK

    g_load = pltpu.make_async_copy(out_grad, g_vmem, local.at[0])
    o_load = pltpu.make_async_copy(output, o_vmem, local.at[1])
    g_load.start()
    o_load.start()
    enter(base, mine, sub, ranges, parts)

    def cut(ref, r, c, size):
        first = pl.multiple_of(r * (ref.shape[1] // ranges) + c * size, size)
        return ref.at[:, pl.ds(first, size)]

    def sends(kind, source, target):
        out = []
        for d in range(1, ranges):
            peer = (mine + d) % ranges
            out.append(
                pltpu.make_async_remote_copy(
                    src_ref=source(peer), dst_ref=target,
                    send_sem=r_send.at[kind, d - 1], recv_sem=r_recv.at[kind, d - 1],
                    device_id=(base + peer, sub), device_id_type=MESH,
                )
            )
        own = pltpu.make_async_copy(source(mine), target, local.at[2 + kind])
        for copy in out:
            copy.start()
        own.start()
        return out + [own]

    def kv_sends(c):
        return sends(2 * c, lambda r: cut(key, r, c, HD), kv.at[c, sub, mine, 0]) + sends(
            2 * c + 1, lambda r: cut(value, r, c, HD), kv.at[c, sub, mine, 1]
        )

    def qg_sends(u):
        kind = 2 * chunks + 2 * u
        return sends(kind, lambda r: cut(query, r, u, columns), qg.at[u, mine, 0]) + sends(
            kind + 1, lambda r: cut(out_grad, r, u, columns), qg.at[u, mine, 1]
        )

    def z_copy(src, dst, send, recv, z):
        return pltpu.make_async_remote_copy(
            src_ref=src, dst_ref=dst, send_sem=send, recv_sem=recv,
            device_id=(base + mine, z), device_id_type=MESH,
        )

    def gather_copy(c, z, d, to, whole):
        ref = kv.at[c, z] if whole else kv.at[c, z, pl.ds(0, ranges - 1)]
        return z_copy(ref, ref, z_send.at[c, d - 1], z_recv.at[c, d - 1], to)

    def forward_copy(c):
        return z_copy(kv.at[c, 0], kv.at[c, 0], relay_send.at[c], z_recv.at[c, parts - 2], 3)

    def gather(c):
        for d in range(1, parts):
            peer = (sub + d) % parts
            far = relay and d == parts - 1

            @pl.when((peer > sub) & (not far))
            def _():
                gather_copy(c, sub, d, peer, True).start()

            @pl.when(peer < sub)
            def _():
                gather_copy(c, sub, d, peer, False).start()

    def forward(c):
        if relay:

            @pl.when(sub == 2)
            def _():
                gather_copy(c, 0, 2, 3, True).wait_recv()
                forward_copy(c).start()

    def gathered(c):
        for d in range(1, parts):
            peer = (sub + d) % parts
            origin = (sub - d + parts) % parts
            far = relay and d == parts - 1
            done = (sub == 2) & (relay and d == 2)

            @pl.when((peer > sub) & (not far))
            def _():
                gather_copy(c, sub, d, peer, True).wait_send()

            @pl.when(peer < sub)
            def _():
                gather_copy(c, sub, d, peer, False).wait_send()

            @pl.when((origin < sub) & jnp.logical_not(done))
            def _():
                gather_copy(c, origin, d, peer, True).wait_recv()

            @pl.when(origin > sub)
            def _():
                gather_copy(c, origin, d, peer, False).wait_recv()

        if relay:

            @pl.when(sub == 2)
            def _():
                forward_copy(c).wait_send()

    def wait(copies):
        for copy in copies:
            copy.wait()

    kv_moves = [kv_sends(0)]
    keep_moves = sends(2 * chunks + 2 * units + 1, lambda r: block_keep, keep_in.at[mine])
    qg_moves = [qg_sends(0)] + [None] * (units - 1)
    wait(kv_moves[0])
    kv_moves += [kv_sends(c) for c in range(1, chunks)]
    gather(0)
    for c in range(chunks):
        for z in range(1, parts):

            @pl.when(z > sub)
            def _():
                kv[c, z, ranges - 1] = jnp.zeros(kv.shape[3:], bf16)

        for d in range(1, parts):
            origin = (sub - d + parts) % parts

            @pl.when(origin < sub)
            def _():
                partial[c, ranges - 1, d - 1] = jnp.zeros(partial.shape[3:], bf16)

        if relay:

            @pl.when(sub == 0)
            def _():
                partial[c, :, 0] = jnp.zeros((ranges,) + partial.shape[3:], bf16)


    g_load.wait()
    o_load.wait()
    ones = jnp.ones((8, 2 * HD), bf16)
    for head in range(lse_t.shape[0]):
        at = slice(head * HD, (head + 1) * HD)
        product = g_vmem[:, at].astype(f32) * o_vmem[:, at].astype(f32)
        high = product.astype(bf16)
        low = (product - high.astype(f32)).astype(bf16)
        both = jnp.concatenate([high, low], axis=1)
        delta = lax.dot_general(ones, both, nt, preferred_element_type=f32)
        r, c, h = head // (units * group), head // group % units, head % group
        to = slice(h * rows, (h + 1) * rows)
        stats_own[r, c, 0:1, to] = lse_t[head : head + 1, :]
        stats_own[r, c, 1:2, to] = delta[0:1]
    stats_moves = sends(2 * chunks + 2 * units, lambda r: stats_own.at[r], stats.at[mine])

    forward(0)
    wait(keep_moves)
    keep_copy = pltpu.make_async_copy(keep_in, keep, local.at[0])
    keep_copy.start()
    keep_copy.wait()
    for c in range(1, chunks):
        wait(kv_moves[c])
    wait(stats_moves)

    def doc_start(position):
        found = jnp.zeros_like(position)
        start = -(base // ranges) * DOC_MAX
        for d in range(lengths.shape[0]):
            found = jnp.maximum(found, jnp.where(start <= position, start, 0))
            start = start + lengths[d]
        return found

    def compute(u, t):
        first_query = t * range_rows + offset
        query_block = first_query // BLOCK
        row_query = first_query + lax.broadcasted_iota(jnp.int32, (1, width), 1) % rows
        row_start = doc_start(row_query)
        heads = range(group)
        queries = [qg[u, t, 0, :, h * HD : (h + 1) * HD] for h in heads]
        grads = [qg[u, t, 1, :, h * HD : (h + 1) * HD] for h in heads]
        queries = jnp.concatenate(queries, axis=0)
        grads = jnp.concatenate(grads, axis=0)
        dqt_acc[...] = jnp.zeros_like(dqt_acc)

        def pair(p, _):
            j = 2 * p
            at = pl.ds(pl.multiple_of(j * BLOCK, 2 * BLOCK), 2 * BLOCK)
            keys, values, keys_t = k_all[at, :], v_all[at, :], kt_all[:, at]
            drop0 = (1 - keep[t, keep_row, query_block - j]) * FAR
            drop1 = (1 - keep[t, keep_row, jnp.maximum(query_block - j - 1, 0)]) * FAR
            line = lax.broadcasted_iota(jnp.int32, (2 * BLOCK, width), 0)
            key_pos = line + j * BLOCK + jnp.where(line < BLOCK, drop0, drop1)
            allowed = (key_pos <= row_query) & (key_pos >= row_start)
            probs_all, dscores_all = [], []
            for first in range(0, total, width):
                q = queries[first : first + width]
                g = grads[first : first + width]
                s = lax.dot_general(keys, q, nt, preferred_element_type=f32)
                dp = lax.dot_general(values, g, nt, preferred_element_type=f32)
                lse = stats[t, u, 0:1, first : first + width]
                delta = stats[t, u, 1:2, first : first + width]
                probs = jnp.where(allowed, jnp.exp2(s * (scale * LOG2E) - lse), 0.0)
                dscores = probs * (dp - delta)
                probs_all.append(probs.astype(bf16))
                dscores_all.append(dscores.astype(bf16))
            probs_all = jnp.concatenate(probs_all, axis=1)
            dscores_all = jnp.concatenate(dscores_all, axis=1)
            dv_acc[at, :] += jnp.dot(probs_all, grads, preferred_element_type=f32)
            dk_acc[at, :] += jnp.dot(dscores_all, queries, preferred_element_type=f32)
            dqt_acc[...] += jnp.dot(keys_t, dscores_all, preferred_element_type=f32)
            return 0

        lax.fori_loop(0, (query_block + 2) // 2, pair, 0)
        for first in range(0, total, width):
            dq = (dqt_acc[:, first : first + width] * scale).T.astype(bf16)
            for h in range(width // rows):
                head = first // rows + h
                dq_out[u, t, :, head * HD : (head + 1) * HD] = dq[h * rows : (h + 1) * rows]

    def store(c, t):
        for z in range(parts):
            first = (t * parts + z) * rows
            dkv_out[c, t, z, 0] = (dk_acc[first : first + rows, :] * scale).astype(bf16)
            dkv_out[c, t, z, 1] = dv_acc[first : first + rows, :].astype(bf16)

    def to_range(t, source, ref, c, size, send, recv, own):
        remote = pltpu.make_async_remote_copy(
            src_ref=source, dst_ref=cut(ref, mine, c, size),
            send_sem=send.at[t], recv_sem=recv.at[mine],
            device_id=(base + t, sub), device_id_type=MESH,
        )
        here = pltpu.make_async_copy(source, cut(ref, mine, c, size), own)

        @pl.when(t != mine)
        def _():
            remote.start()

        @pl.when(t == mine)
        def _():
            here.start()

        def finish():
            @pl.when(t != mine)
            def _():
                remote.wait_send()
                pltpu.make_async_remote_copy(
                    src_ref=source, dst_ref=cut(ref, t, c, size),
                    send_sem=send.at[t], recv_sem=recv.at[t],
                    device_id=(base + t, sub), device_id_type=MESH,
                ).wait_recv()

            @pl.when(t == mine)
            def _():
                here.wait()

        return finish

    def partial_copy(c, t, d, peer):
        return z_copy(
            dkv_out.at[c, t, peer], partial.at[c, t, d - 1],
            p_send.at[c, t, d - 1], p_recv.at[c, t, d - 1], peer,
        )

    def far_copy(c, t):
        return z_copy(
            dkv_out.at[c, t, 0], relayed.at[c, t],
            p_send.at[c, t, 0], relay_recv.at[c, t], 2,
        )

    def is_sent(t, d, peer, origin):
        sent = (peer < origin) | (t < ranges - 1)
        if relay and d == 1:
            sent = sent & (origin != 3)
        return sent

    def send_partial(c, t):
        for d in range(1, parts):
            peer = (sub + d) % parts
            late = (sub == 2) & (relay and d == 2)

            @pl.when(is_sent(t, d, peer, sub) & jnp.logical_not(late))
            def _():
                partial_copy(c, t, d, peer).start()

        if relay:

            @pl.when(sub == 3)
            def _():
                far_copy(c, t).start()

    def send_late(c, t):
        if relay:

            @pl.when(sub == 2)
            def _():
                far_copy(c, t).wait_recv()
                both = dkv_out[c, t, 0].astype(f32) + relayed[c, t].astype(f32)
                dkv_out[c, t, 0] = both.astype(bf16)
                partial_copy(c, t, 2, 0).start()

    def sent_partial(c, t):
        for d in range(1, parts):
            peer = (sub + d) % parts

            @pl.when(is_sent(t, d, peer, sub))
            def _():
                partial_copy(c, t, d, peer).wait_send()

        if relay:

            @pl.when(sub == 3)
            def _():
                far_copy(c, t).wait_send()

    def add_up(c, t):
        for d in range(1, parts):
            origin = (sub - d + parts) % parts

            @pl.when(is_sent(t, d, sub, origin))
            def _():
                partial_copy(c, t, d, (sub + d) % parts).wait_recv()

        for part in range(2):
            sums = dkv_out[c, t, sub, part].astype(f32)
            for d in range(parts - 1):
                sums += partial[c, t, d, part].astype(f32)
            summed[c, t, part] = sums.astype(bf16)
        for part, ref in enumerate((key_grad, value_grad)):
            finishes.append(
                to_range(
                    t, summed.at[c, t, part], ref, c, HD,
                    f_send.at[c, part], f_recv.at[c, part], f_own.at[c, part],
                )
            )

    finishes = []
    order = list(range(ranges - 1, -1, -1))
    late, ready = [], []

    def send_dq(u, t):
        finishes.append(
            to_range(
                t, dq_out.at[u, t], query_grad, u, columns,
                q_send.at[u], q_recv.at[u], q_own.at[u],
            )
        )

    for u in range(units):
        c = u // halves
        wait(qg_moves[u])
        if u + 1 < units:
            qg_moves[u + 1] = qg_sends(u + 1)
        for held in order if u > 0 else ():
            send_dq(u - 1, held)
        if u % halves == 0:
            gathered(c)
            if c + 1 < chunks:
                gather(c + 1)
            for t in range(ranges):
                for z in range(parts):
                    first = (t * parts + z) * rows
                    k_all[first : first + rows, :] = kv[c, z, t, 0]
                    v_all[first : first + rows, :] = kv[c, z, t, 1]
            for first in range(0, span, 256):
                piece = k_all[first : first + 256, :].astype(f32)
                kt_all[:, first : first + 256] = piece.T.astype(bf16)
            dk_acc[...] = jnp.zeros_like(dk_acc)
            dv_acc[...] = jnp.zeros_like(dv_acc)
        for i, t in enumerate(order):
            compute(u, t)
            if u == units - 1:
                send_dq(u, t)
            if u % halves == halves - 1:
                store(c, t)
                send_partial(c, t)
                late.append((c, t))
            if len(late) > 1:
                at = late.pop(0)
                send_late(*at)
                ready.append(at)
            if len(ready) > ranges - 1:
                add_up(*ready.pop(0))
            if i == 1 and u % halves == 0 and c + 1 < chunks:
                forward(c + 1)
    for at in late:
        send_late(*at)
        ready.append(at)
    for at in ready:
        add_up(*at)
    for c in range(chunks):
        for t in order:
            sent_partial(c, t)
    for finish in finishes:
        finish()


def shards(query, key, value, output, out_grad, lse, doc_lengths, block_keep):
    rows, wide = query.shape
    narrow = key.shape[1]
    parts = lax.axis_size("head")
    range_rows = rows * parts
    ranges = DOC_MAX // range_rows
    chunks = KVH // ranges
    units = chunks
    columns = wide // (ranges * units)
    total = columns // HD * rows
    f32, bf16 = jnp.float32, jnp.bfloat16
    anywhere = pl.BlockSpec(memory_space=pl.ANY)
    vmem, dma = pltpu.VMEM, pltpu.SemaphoreType.DMA
    kinds = 2 * chunks + 2 * units + 2
    return pl.pallas_call(
        functools.partial(whole_kernel, ranges, parts),
        out_shape=(
            jax.ShapeDtypeStruct((rows, wide), bf16),
            jax.ShapeDtypeStruct((rows, narrow), bf16),
            jax.ShapeDtypeStruct((rows, narrow), bf16),
        ),
        in_specs=[pl.BlockSpec(memory_space=pltpu.SMEM)]
        + [anywhere] * 5
        + [pl.BlockSpec(memory_space=pltpu.VMEM), anywhere],
        out_specs=(anywhere,) * 3,
        scratch_shapes=[
            vmem((rows, wide), bf16),
            vmem((rows, wide), bf16),
            vmem((ranges, units, 2, total), f32),
            vmem((ranges, units, 2, total), f32),
            vmem((units, ranges, 2, rows, columns), bf16),
            vmem((chunks, parts, ranges, 2, rows, HD), bf16),
            vmem((ranges,) + block_keep.shape, jnp.int32),
            pltpu.SMEM((ranges,) + block_keep.shape, jnp.int32),
            vmem((DOC_MAX, HD), bf16),
            vmem((DOC_MAX, HD), bf16),
            vmem((HD, DOC_MAX), bf16),
            vmem((DOC_MAX, HD), f32),
            vmem((DOC_MAX, HD), f32),
            vmem((HD, total), f32),
            vmem((units, ranges, rows, columns), bf16),
            vmem((chunks, ranges, parts, 2, rows, HD), bf16),
            vmem((chunks, ranges, parts - 1, 2, rows, HD), bf16),
            vmem((chunks, ranges, 2, rows, HD), bf16),
            dma((2 + kinds,)),
            dma((kinds, ranges - 1)),
            dma((kinds, ranges - 1)),
            dma((chunks, parts - 1)),
            dma((chunks, parts - 1)),
            dma((units, ranges)),
            dma((units, ranges)),
            dma((chunks, ranges, parts - 1)),
            dma((chunks, ranges, parts - 1)),
            dma((chunks, 2, ranges)),
            dma((chunks, 2, ranges)),
            vmem((chunks, ranges, 2, rows, HD), bf16),
            dma((chunks,)),
            dma((chunks, ranges)),
            dma((units,)),
            dma((chunks, 2)),
        ],
        compiler_params=pltpu.CompilerParams(
            collective_id=0, has_side_effects=True, vmem_limit_bytes=60 * 1024 * 1024
        ),
        cost_estimate=pl.CostEstimate(
            flops=10 * total * DOC_MAX * HD * ranges * chunks // 2,
            bytes_accessed=7 * rows * wide * 2,
            transcendentals=total * DOC_MAX * ranges * chunks // 2,
        ),
    )(doc_lengths, query, key, value, output, out_grad, (lse * LOG2E).T, block_keep)


def solution(mesh):
    tokens = P(("blk", "head"), None)
    in_specs = (tokens, tokens, tokens, tokens, tokens, tokens, P(), P("blk", None))
    out_specs = (tokens, tokens, tokens)
    return jax.shard_map(shards, mesh=mesh, in_specs=in_specs, out_specs=out_specs, check_vma=False)
```
